32 devices in a mesh: dp: 8 (over y, x, core), tensor: 4 (over z).
Axes of the slice: x: 2, y: 2, z: 4, core: 2. Of those that a mesh axis runs over, the one named last changes fastest.
Arguments:
- qkv: bfloat16 [4, 640, 3, 4096], P(None, 'dp', None, 'tensor'), may hold values from -6 to 6
- fir_buffer: bfloat16 [640, 3, 2, 4096], P('dp', None, None, 'tensor'), may hold values from -6 to 6
- fir_taps: float32 [3, 3, 4096], P(None, None, 'tensor'), may hold values from -3 to 3
- modal_state: float32 [640, 16, 4096], P('dp', None, 'tensor'), may hold values from -6 to 6
- poles: float32 [16, 4096], P(None, 'tensor'), may hold values from 0.5 to 0.999
- residues: float32 [16, 4096], P(None, 'tensor'), may hold values from -1.5 to 1.5
- skip: float32 [4096], P('tensor'), may hold values from -3 to 3
- out_weight: bfloat16 [4096, 4096], P('tensor')
- norm_gain: float32 [4096], P('tensor'), may hold values from 0.25 to 1.75
- finished: int32 [3, 640], P(None, 'dp'), may hold values 0 or 1
- dest_group: int32 [3, 640], P(None, 'dp'), may hold values from 0 to 7, as said below
Outputs:
- mixed: bfloat16 [4, 640, 4096], P(None, 'dp', 'tensor')
- final_state: float32 [640, 16, 4096], P('dp', None, 'tensor')
- final_lagged: bfloat16 [640, 3, 2, 4096], P('dp', None, None, 'tensor')
The draws below stay inside these ranges and needn't reach their ends.
Inputs may be any that keep to these rules, and one draw needn't show every extreme that they name: `dest_group`: for each migration, the slots s < 16 of every group form bands of 2 slots; all rows of band b of group g go to group (g + k_b) mod 8, where k_b is the same for every group and takes each value of 0 to 7 for exactly one band. Rows in later slots stay. So each group sends exactly 2 rows to every group and the moves are a permutation of the rows.
All inputs are finite; a program needn't handle non-finite values. No bound on the sum of `finished` on one device may be relied on, other than what follows from the above.
Results may differ from the reference program's by a relative error of at most 0.0048.
Values may be sent and summed in bfloat16 or wider, within the bound.
A program may use at most 128 MiB of HBM per device.

```python
import math
import jax
import jax.numpy as jnp
from jax import lax

C = 4096
DOUT = 4096
ORDER = 16
TAPS = 3
STEPS = 4
CAP = 2
ROWS_DEV = 80
MIGS = 3
ROWS = 640


def draw_out_weight(key, part):
    key = jax.random.fold_in(key, 11)
    columns = jnp.arange(DOUT, dtype=jnp.float32) / DOUT
    col_scale = jnp.exp(columns * math.log(10.0)) * (0.25 / math.sqrt(C))
    noise = jax.random.normal(key, (C, DOUT), jnp.float32)
    return (noise * col_scale[None, :]).astype(jnp.bfloat16)


def draw_dest_group(key, part):
    key = jax.random.fold_in(key, 7)
    groups = ROWS // ROWS_DEV
    row_index = jnp.arange(ROWS, dtype=jnp.int32)
    home_group = row_index // ROWS_DEV
    slot_index = row_index % ROWS_DEV
    band_index = jnp.minimum(slot_index // CAP, groups - 1)
    moving = slot_index < groups * CAP
    plans = []
    for turn_index in range(MIGS):
        shifts = jax.random.permutation(jax.random.fold_in(key, turn_index), groups).astype(jnp.int32)
        plans.append(jnp.where(moving, (home_group + shifts[band_index]) % groups, home_group))
    return jnp.stack(plans).astype(jnp.int32)


def touch_ends(result, stream_key, smallest, high):
    longest = result.shape.index(max(result.shape))
    spots = []
    for shift in (0, 1):
        where = [jax.random.randint(jax.random.fold_in(stream_key, axis), (), 0, length) for axis, length in enumerate(result.shape)]
        where[longest] = (where[longest] + shift) % result.shape[longest]
        spots.append(tuple(where))
    return result.at[spots[0]].set(smallest).at[spots[1]].set(high)


def level_of(own_key, extent, shards, low, largest):
    loudness = 1.0
    for axis_at, shards_of in shards:
        steps = jax.random.uniform(jax.random.fold_in(jax.random.fold_in(own_key, 6), axis_at), (shards_of,), jnp.float32, low / len(shards), largest / len(shards))
        loudness = loudness * jnp.repeat(jnp.exp(steps), extent[axis_at] // shards_of).reshape((-1,) + (1,) * (len(extent) - 1 - axis_at))
    return loudness


def gaussian(stream_key, shape, spread, reach, pieces=(), kind=jnp.bfloat16):
    values = jax.random.normal(stream_key, shape, jnp.float32) * spread
    if len(pieces) > 0:
        values = level_of(stream_key, shape, pieces, -0.22, 0.18) * values
    return jnp.clip(values, min=-reach, max=reach).astype(kind)


def setup_inputs(seed: int = 0) -> dict:
    arg_keys = jax.random.split(jax.random.key(seed), 12)
    qkv = gaussian(arg_keys[0], (STEPS, ROWS, 3, C), 1.0, 6.0, ((1, 8), (3, 4)))
    fir_buffer = gaussian(arg_keys[1], (ROWS, 3, 2, C), 1.0, 6.0, ((0, 8), (3, 4)))
    fir_taps = gaussian(arg_keys[2], (3, TAPS, C), 0.6, 3.0, ((2, 4),), jnp.float32)
    modal_state = gaussian(arg_keys[3], (ROWS, ORDER, C), 1.0, 6.0, ((0, 8), (2, 4)), jnp.float32)
    poles = jnp.clip(0.5 + 0.499 * jax.random.uniform(arg_keys[4], (ORDER, C), jnp.float32) ** level_of(arg_keys[4], (ORDER, C), ((1, 4),), -0.2, 0.2), 0.5, 0.999)
    residues = gaussian(arg_keys[5], (ORDER, C), 0.25, 1.5, ((1, 4),), jnp.float32)
    skip = gaussian(arg_keys[6], (C,), 0.5, 3.0, ((0, 4),), jnp.float32)
    out_weight = draw_out_weight(jax.random.fold_in(arg_keys[11], 71), 0)
    norm_gain = jnp.clip(1.0 + 0.15 * jax.random.normal(arg_keys[8], (DOUT,), jnp.float32), 0.25, 1.75)
    finished = touch_ends((jax.random.randint(arg_keys[9], (MIGS, ROWS), 0, 4) < 1).astype(jnp.int32), jax.random.fold_in(arg_keys[9], 1), 0, 1)
    dest_group = draw_dest_group(jax.random.fold_in(arg_keys[11], 71), 0)
    return dict(qkv=qkv, fir_buffer=fir_buffer, fir_taps=fir_taps, modal_state=modal_state, poles=poles, residues=residues, skip=skip, out_weight=out_weight, norm_gain=norm_gain, finished=finished, dest_group=dest_group)


def reference(qkv, fir_buffer, fir_taps, modal_state, poles, residues, skip, out_weight, norm_gain, finished, dest_group):
    state_now = modal_state
    lagged = fir_buffer
    slot_index = jnp.arange(ROWS, dtype=jnp.int32) % ROWS_DEV
    results = []
    for turn_index in range(STEPS):
        incoming = qkv[turn_index]
        filtered = fir_taps[None, :, 0, :] * incoming.astype(jnp.float32)
        filtered = filtered + fir_taps[None, :, 1, :] * lagged[:, :, 0, :].astype(jnp.float32)
        filtered = filtered + fir_taps[None, :, 2, :] * lagged[:, :, 1, :].astype(jnp.float32)
        lagged = jnp.stack([incoming, lagged[:, :, 0, :]], axis=2)
        product = filtered[:, 1] * filtered[:, 2]
        state_now = poles[None] * state_now + product[:, None, :]
        modal_out = lax.optimization_barrier(jnp.sum(residues[None] * state_now, axis=1)) + skip[None] * product
        gated_out = (filtered[:, 0] * modal_out).astype(jnp.bfloat16)
        projected = jnp.dot(gated_out, out_weight, preferred_element_type=jnp.float32)
        norm_scale = lax.rsqrt(lax.optimization_barrier(jnp.mean(projected * projected, axis=1, keepdims=True)) + 1e-05)
        results.append((projected * norm_scale * norm_gain[None]).astype(jnp.bfloat16))
        if turn_index < STEPS - 1:
            alive = (1 - finished[turn_index]).astype(jnp.float32)
            target = (dest_group[turn_index] * ROWS_DEV + slot_index).astype(jnp.int32)
            state_now = jnp.zeros_like(state_now).at[target].set(state_now * alive[:, None, None])
            lagged = jnp.zeros_like(lagged).at[target].set(lagged * alive.astype(jnp.bfloat16)[:, None, None, None])
    return (jnp.stack(results), state_now, lagged)
```

```python
import functools

import jax
import jax.numpy as jnp
from jax import lax
from jax.experimental import pallas as pl
from jax.experimental.pallas import tpu as pltpu
from jax.sharding import PartitionSpec as P

STEPS = 4
CAP = 2
MESH = pl.DeviceIdType.MESH
LANES = 512


def row_update(poles, res, skip, s, x, p):
    s = poles * s + p
    y = jnp.sum(res * s, axis=0, keepdims=True) + skip * p
    return s, x * y


def kernel(groups, shards, chunks, *refs):
    refs = list(refs)

    def take(count):
        got = refs[:count]
        del refs[:count]
        return got

    nc = len(chunks)
    q_ref, l_ref, qm_ref, lm_ref, tap_ref, tapm_ref, mask_ref = take(7)
    st_ref, pole_ref, res_ref, skip_ref, w_hbm, gain_ref = take(6)
    alive_ref, bandfor_ref, shift_ref = take(3)
    mix_refs, st_outs = take(nc), take(nc)
    (lag_out,) = take(1)
    s_refs = take(nc)
    w_ref, lagm, msend = take(3)
    mrecv = take(STEPS - 1)
    gm, xs, ps, ys = take(4)
    g_refs, p_refs, r_refs, t_refs = take(nc), take(nc), take(nc), take(nc)
    ss_own, ss_recv = take(2)
    load_sem, store_sem, ms_sem, mr_sem, rs_sem, rr_sem, ss_sem, sr_sem = take(8)
    sm = s_refs[0]
    me = lax.axis_index("dp")
    z = lax.axis_index("tensor")
    cols = gain_ref.shape[1]
    chans = pole_ref.shape[1]
    lanes = min(LANES, chans)
    blocks = [slice(i, i + lanes) for i in range(0, chans, lanes)]
    bands_m = chunks[0] // CAP
    firsts = [sum(chunks[:c]) for c in range(nc)]
    parity = lax.broadcasted_iota(jnp.int32, (8, lanes), 0) % 2

    barrier = pltpu.get_barrier_semaphore()

    @pl.loop(1, groups)
    def _(d):
        pl.semaphore_signal(barrier, inc=1, device_id={"dp": lax.rem(me + d, groups)}, device_id_type=MESH)

    @pl.loop(1, shards)
    def _(d):
        pl.semaphore_signal(barrier, inc=1, device_id={"tensor": lax.rem(z + d, shards)}, device_id_type=MESH)

    loads = [
        pltpu.make_async_copy(st_ref.at[pl.ds(firsts[c], chunks[c])], s_refs[c], load_sem.at[c])
        for c in range(nc)
    ]
    load_w = pltpu.make_async_copy(w_hbm, w_ref, load_sem.at[nc])
    stores = [pltpu.make_async_copy(s_refs[c], st_outs[c], store_sem.at[c]) for c in range(nc)]
    loads[0].start()
    loads[1].start()
    load_w.start()
    for load in loads[2:]:
        load.start()
    ss_own[...] = jnp.zeros_like(ss_own)

    def migration(turn, d):
        return pltpu.make_async_remote_copy(
            src_ref=msend.at[turn, d],
            dst_ref=mrecv[turn].at[d],
            send_sem=ms_sem.at[turn, d],
            recv_sem=mr_sem.at[turn, d],
            device_id={"dp": lax.rem(me + d, groups)},
            device_id_type=MESH,
        )

    def filtered(sl, q, one, two):
        return tapm_ref[0, :, sl] * q + tapm_ref[1, :, sl] * one + tapm_ref[2, :, sl] * two

    def moving_step(turn):
        @pl.loop(0, bands_m)
        def _(b):
            for sl in blocks:
                q = qm_ref[turn, b, :, sl]
                if turn == 0:
                    one = lm_ref[0, b, :, sl]
                    two = lm_ref[1, b, :, sl]
                    states = [sm[b * CAP + r, :, sl] for r in range(CAP)]
                else:
                    k = shift_ref[turn - 1, b]
                    states = [
                        mrecv[turn - 1][k, 16 * r : 16 * r + 16, sl].astype(jnp.float32)
                        for r in range(CAP)
                    ]
                    lags = mrecv[turn - 1][k, 32:48, sl].astype(jnp.float32)
                    one = lags[:8]
                    two = lags[8:]
                f = filtered(sl, q, one, two)
                for r in range(CAP):
                    p = f[2 + r : 3 + r] * f[4 + r : 5 + r]
                    s, g = row_update(
                        pole_ref[:, sl], res_ref[:, sl], skip_ref[:, sl], states[r], f[r : r + 1], p
                    )
                    gm[pl.ds(turn * chunks[0] + b * CAP + r, 1), sl] = g
                    if turn < STEPS - 1:
                        s = s * alive_ref[turn, b * CAP + r]
                    sm[b * CAP + r, :, sl] = s
                if turn < STEPS - 1:
                    mask = jnp.where(
                        parity == 0, alive_ref[turn, b * CAP], alive_ref[turn, b * CAP + 1]
                    )
                    lagm[b, 0:8, sl] = q * mask
                    lagm[b, 8:16, sl] = one * mask
                else:
                    lag_out[b, :, sl] = one

    def pack(turn, d, to_ref):
        b = bandfor_ref[turn, d]
        for r in range(CAP):
            to_ref[16 * r : 16 * r + 16, :] = sm[b * CAP + r].astype(jnp.bfloat16)
        to_ref[32:48, :] = lagm[b].astype(jnp.bfloat16)

    def send_moving(turn):
        pack(turn, 0, mrecv[turn].at[0])

        @pl.loop(1, groups)
        def _(d):
            pack(turn, d, msend.at[turn, d])
            migration(turn, d).start()

    def await_moving(turn):
        @pl.loop(1, groups)
        def _(d):
            migration(turn, d).wait_recv()

    def staying(c):
        rows, first, s_ref, g_ref = chunks[c], firsts[c], s_refs[c], g_refs[c]

        @pl.loop(0, rows // 16)
        def _(i):
            at = pl.multiple_of(first + i * 16, 16)
            lag_at = pl.multiple_of(at - chunks[0], 16)

            @pl.loop(0, chans // 128)
            def _(block):
                sl = pl.ds(pl.multiple_of(block * 128, 128), 128)
                one = [l_ref[0, j, pl.ds(lag_at, 16), sl].astype(jnp.float32) for j in range(3)]
                two = [l_ref[1, j, pl.ds(lag_at, 16), sl].astype(jnp.float32) for j in range(3)]
                for turn in range(STEPS):
                    q = [q_ref[turn, j, pl.ds(at, 16), sl].astype(jnp.float32) for j in range(3)]
                    f = [
                        tap_ref[j, 0:1, sl] * q[j]
                        + tap_ref[j, 1:2, sl] * one[j]
                        + tap_ref[j, 2:3, sl] * two[j]
                        for j in range(3)
                    ]
                    xs[turn, :, sl] = f[0]
                    ps[turn, :, sl] = f[1] * f[2]
                    if turn < STEPS - 1:
                        mask = mask_ref[turn, pl.ds(at, 16), :]
                        two = [v * mask for v in one]
                        one = [v * mask for v in q]

            @pl.loop(0, 16)
            def _(r):
                for sl in blocks:
                    s = s_ref[i * 16 + r, :, sl]
                    for turn in range(STEPS):
                        s = pole_ref[:, sl] * s + ps[turn, pl.ds(r, 1), sl]
                        ys[turn, pl.ds(r, 1), sl] = jnp.sum(res_ref[:, sl] * s, axis=0, keepdims=True)
                        if turn < STEPS - 1:
                            s = s * alive_ref[turn, at + r]
                    s_ref[i * 16 + r, :, sl] = s

            for turn in range(STEPS):
                g_ref[pl.ds(pl.multiple_of(turn * rows + i * 16, 16), 16), :] = (
                    xs[turn] * (ys[turn] + skip_ref[...] * ps[turn])
                ).astype(jnp.bfloat16)

    def part_copy(c, j):
        return pltpu.make_async_remote_copy(
            src_ref=p_refs[c].at[j],
            dst_ref=r_refs[c].at[j],
            send_sem=rs_sem.at[c, j],
            recv_sem=rr_sem.at[c, j],
            device_id={"tensor": lax.rem(z + j, shards)},
            device_id_type=MESH,
        )

    def project(c):
        g_ref, p_ref, t_ref = g_refs[c], p_refs[c], t_refs[c]

        def product(j):
            owner = lax.rem(z + j, shards)
            return jnp.dot(
                g_ref[...],
                w_ref[:, pl.ds(pl.multiple_of(owner * cols, cols), cols)],
                preferred_element_type=jnp.float32,
            )

        @pl.loop(1, shards)
        def _(j):
            p_ref[j] = product(j).astype(jnp.bfloat16)
            part_copy(c, j).start()

        t_ref[...] = product(0)

    def pieces(rows):
        return [(i, min(128, rows - i)) for i in range(0, rows, 128)]

    def eye(size):
        return lax.broadcasted_iota(jnp.int32, (size, 128), 0) == lax.broadcasted_iota(
            jnp.int32, (size, 128), 1
        )

    def square_copy(c, j):
        return pltpu.make_async_remote_copy(
            src_ref=ss_own.at[c],
            dst_ref=ss_recv.at[c, j],
            send_sem=ss_sem.at[c, j],
            recv_sem=sr_sem.at[c, j],
            device_id={"tensor": lax.rem(z + j, shards)},
            device_id_type=MESH,
        )

    def collect(c):
        r_ref, t_ref = r_refs[c], t_refs[c]
        for j in range(1, shards):
            part_copy(c, j).wait_recv()
        for at, (i, size) in enumerate(pieces(t_ref.shape[0])):
            x = t_ref[i : i + size, :]
            for j in range(1, shards):
                x = x + r_ref[j, i : i + size, :].astype(jnp.float32)
            t_ref[i : i + size, :] = x
            squares = jnp.sum(x * x, axis=1, keepdims=True)
            ss_own[c, at : at + 1, :] = jnp.sum(
                jnp.where(eye(size), squares, 0.0), axis=0, keepdims=True
            )
        for j in range(1, shards):
            square_copy(c, j).start()

    def finish(c):
        t_ref, out_ref = t_refs[c], mix_refs[c]
        for j in range(1, shards):
            square_copy(c, j).wait_recv()
        total = ss_own[c]
        for j in range(1, shards):
            total = total + ss_recv[c, j]
        for at, (i, size) in enumerate(pieces(t_ref.shape[0])):
            squares = jnp.sum(jnp.where(eye(size), total[at : at + 1], 0.0), axis=1, keepdims=True)
            scale = lax.rsqrt(squares / (cols * shards) + 1e-05)
            out_ref[i : i + size, :] = (t_ref[i : i + size, :] * scale * gain_ref[...]).astype(
                jnp.bfloat16
            )

    def stay(c):
        loads[c].wait()
        staying(c)
        stores[c].start()
        if c == 1:
            load_w.wait()
        project(c)

    loads[0].wait()
    moving_step(0)
    pl.semaphore_wait(barrier, groups + shards - 2)
    send_moving(0)
    stay(1)
    await_moving(0)
    moving_step(1)
    send_moving(1)
    for c in range(2, nc):
        stay(c)
    await_moving(1)
    moving_step(2)
    send_moving(2)
    await_moving(2)
    moving_step(3)
    stores[0].start()
    g_refs[0][...] = gm[...].astype(jnp.bfloat16)
    project(0)
    for c in range(1, nc):
        collect(c)
    for c in range(1, nc):
        finish(c)
    collect(0)
    finish(0)
    for turn in range(STEPS - 1):
        @pl.loop(1, groups)
        def _(d):
            migration(turn, d).wait_send()
    for j in range(1, shards):
        for c in range(nc):
            part_copy(c, j).wait_send()
            square_copy(c, j).wait_send()
    for store in stores:
        store.wait()


def per_device(
    qkv,
    fir_buffer,
    fir_taps,
    modal_state,
    poles,
    residues,
    skip,
    out_weight,
    norm_gain,
    finished,
    dest_group,
):
    groups = lax.axis_size("dp")
    shards = lax.axis_size("tensor")
    rows, order, chans = modal_state.shape
    cols = norm_gain.shape[0]
    me = lax.axis_index("dp")
    f32 = jnp.float32
    bf16 = jnp.bfloat16

    moving = groups * CAP
    q_bands = qkv[:, :moving].reshape(STEPS, groups, CAP, 3, chans).transpose(0, 1, 3, 2, 4)
    q_bands = q_bands.reshape(STEPS, groups, 3 * CAP, chans).astype(f32)
    q_bands = jnp.pad(q_bands, ((0, 0), (0, 0), (0, 2), (0, 0)))
    l_bands = fir_buffer[:moving].reshape(groups, CAP, 3, 2, chans).transpose(3, 0, 2, 1, 4)
    l_bands = l_bands.reshape(2, groups, 3 * CAP, chans).astype(f32)
    l_bands = jnp.pad(l_bands, ((0, 0), (0, 0), (0, 2), (0, 0)))
    taps = jnp.repeat(fir_taps.transpose(1, 0, 2), CAP, axis=1)
    taps = jnp.pad(taps, ((0, 0), (0, 2), (0, 0)))
    alive = (1 - finished).astype(f32)
    mask = jnp.broadcast_to(alive[:, :, None], alive.shape + (128,))
    shift = (dest_group[:, 0:moving:CAP] - me + groups) % groups
    ids = jnp.arange(groups, dtype=jnp.int32)
    bandfor = jnp.sum(jnp.where(shift[:, None, :] == ids[None, :, None], ids[None, None, :], 0), axis=2)

    left = rows - moving
    half = left // 32 * 16
    chunks = (moving,) + ((half, left - half) if half else (left,))
    nc = len(chunks)
    tall = [STEPS * n for n in chunks]
    vmem = pl.BlockSpec(memory_space=pltpu.VMEM)
    smem = pl.BlockSpec(memory_space=pltpu.SMEM)
    hbm = pl.BlockSpec(memory_space=pl.ANY)
    dma = pltpu.SemaphoreType.DMA
    outs = pl.pallas_call(
        functools.partial(kernel, groups, shards, chunks),
        out_shape=[jax.ShapeDtypeStruct((n, cols), bf16) for n in tall]
        + [jax.ShapeDtypeStruct((n, order, chans), f32) for n in chunks]
        + [jax.ShapeDtypeStruct((groups, 8, chans), f32)],
        in_specs=[vmem] * 7 + [hbm, vmem, vmem, vmem, hbm, vmem, smem, smem, smem],
        out_specs=[vmem] * nc + [hbm] * nc + [vmem],
        scratch_shapes=[pltpu.VMEM((n, order, chans), f32) for n in chunks]
        + [
            pltpu.VMEM(out_weight.shape, bf16),
            pltpu.VMEM((groups, 16, chans), f32),
            pltpu.VMEM((STEPS - 1, groups, 48, chans), bf16),
        ]
        + [pltpu.VMEM((groups, 48, chans), bf16)] * (STEPS - 1)
        + [pltpu.VMEM((tall[0], chans), f32)]
        + [pltpu.VMEM((STEPS, 16, chans), f32)] * 3
        + [pltpu.VMEM((n, chans), bf16) for n in tall]
        + [pltpu.VMEM((shards, n, cols), bf16) for n in tall]
        + [pltpu.VMEM((shards, n, cols), bf16) for n in tall]
        + [pltpu.VMEM((n, cols), f32) for n in tall]
        + [
            pltpu.VMEM((nc, 8, 128), f32),
            pltpu.VMEM((nc, shards, 8, 128), f32),
            dma((nc + 1,)),
            dma((nc,)),
            dma((STEPS - 1, groups)),
            dma((STEPS - 1, groups)),
            dma((nc, shards)),
            dma((nc, shards)),
            dma((nc, shards)),
            dma((nc, shards)),
        ],
        compiler_params=pltpu.CompilerParams(
            collective_id=0, has_side_effects=True, vmem_limit_bytes=56 * 1024 * 1024
        ),
        name="mixer",
    )(
        qkv.transpose(0, 2, 1, 3),
        fir_buffer[moving:].transpose(2, 1, 0, 3),
        q_bands,
        l_bands,
        fir_taps,
        taps,
        mask,
        modal_state,
        poles,
        residues,
        skip[None],
        out_weight,
        norm_gain[None],
        alive,
        bandfor.astype(jnp.int32),
        shift.astype(jnp.int32),
    )
    mixed = jnp.concatenate([o.reshape(STEPS, -1, cols) for o in outs[:nc]], axis=1)
    state = jnp.concatenate(outs[nc : 2 * nc], axis=0)
    moved = outs[2 * nc][:, : 3 * CAP].reshape(groups, 3, CAP, chans).transpose(0, 2, 1, 3)
    moved = moved.reshape(moving, 3, chans).astype(bf16)
    stayed = qkv[2, moving:] * alive[2, moving:].astype(bf16)[:, None, None]
    lagged = jnp.stack([qkv[3], jnp.concatenate([moved, stayed], axis=0)], axis=2)
    return (mixed, state, lagged)


def solution(mesh):
    return jax.shard_map(
        per_device,
        mesh=mesh,
        in_specs=(
            P(None, "dp", None, "tensor"),
            P("dp", None, None, "tensor"),
            P(None, None, "tensor"),
            P("dp", None, "tensor"),
            P(None, "tensor"),
            P(None, "tensor"),
            P("tensor"),
            P("tensor", None),
            P("tensor"),
            P(None, "dp"),
            P(None, "dp"),
        ),
        out_specs=(P(None, "dp", "tensor"), P("dp", None, "tensor"), P("dp", None, None, "tensor")),
        check_vma=False,
    )
```

```python
import functools

import jax
import jax.numpy as jnp
from jax import lax
from jax.experimental import pallas as pl
from jax.experimental.pallas import tpu as pltpu
from jax.sharding import PartitionSpec as P

STEPS = 4
CAP = 2
MESH = pl.DeviceIdType.MESH
LANES = 512


def row_update(poles, res, skip, s, x, p):
    s = poles * s + p
    y = jnp.sum(res * s, axis=0, keepdims=True) + skip * p
    return s, x * y


def kernel(groups, shards, chunks, *refs):
    refs = list(refs)

    def take(count):
        got = refs[:count]
        del refs[:count]
        return got

    nc = len(chunks)
    q_ref, l_ref, tap_ref, fin_ref = take(4)
    st_ref, pole_ref, res_ref, skip_ref, w_hbm, gain_ref = take(6)
    done_ref, dest_ref = take(2)
    mix_out, st_out, lag_out = take(3)
    s_refs = take(nc)
    w_ref, lagn, lagm, msend = take(4)
    mrecv = take(STEPS - 1)
    xm, pm, ym, xs, ps, ys = take(6)
    g_refs, p_refs, r_refs, relay_refs, t_refs = take(nc), take(nc), take(nc), take(nc), take(nc)
    ss_own, ss_recv = take(2)
    load_sem, store_sem, ms_sem, mr_sem, rs_sem, rr_sem, rl_sem, ss_sem, sr_sem = take(9)
    sm = s_refs[0]
    me = lax.axis_index("dp")
    z = lax.axis_index("tensor")
    cols = gain_ref.shape[1]
    chans = pole_ref.shape[1]
    lanes = min(LANES, chans)
    blocks = [slice(i, i + lanes) for i in range(0, chans, lanes)]
    bands_m = chunks[0] // CAP
    firsts = [sum(chunks[:c]) for c in range(nc)]

    barrier = pltpu.get_barrier_semaphore()

    @pl.loop(1, groups)
    def _(d):
        pl.semaphore_signal(barrier, inc=1, device_id={"dp": lax.rem(me + d, groups)}, device_id_type=MESH)

    @pl.loop(1, shards)
    def _(d):
        pl.semaphore_signal(barrier, inc=1, device_id={"tensor": lax.rem(z + d, shards)}, device_id_type=MESH)

    loads = [
        pltpu.make_async_copy(st_ref.at[pl.ds(firsts[c], chunks[c])], s_refs[c], load_sem.at[c])
        for c in range(nc)
    ]
    load_w = pltpu.make_async_copy(w_hbm, w_ref, load_sem.at[nc])
    stores = [
        pltpu.make_async_copy(s_refs[c], st_out.at[pl.ds(firsts[c], chunks[c])], store_sem.at[c])
        for c in range(nc)
    ]
    loads[0].start()
    loads[1].start()
    load_w.start()
    for load in loads[2:]:
        load.start()
    ss_own[...] = jnp.zeros_like(ss_own)
    lagm[...] = jnp.zeros_like(lagm)

    def migration(turn, d):
        return pltpu.make_async_remote_copy(
            src_ref=msend.at[turn, d],
            dst_ref=mrecv[turn].at[d],
            send_sem=ms_sem.at[turn, d],
            recv_sem=mr_sem.at[turn, d],
            device_id={"dp": lax.rem(me + d, groups)},
            device_id_type=MESH,
        )

    def alive(turn, row):
        return (1 - done_ref[turn, row]).astype(jnp.float32)

    def alive_column(turn, at):
        shape = (16, fin_ref.shape[1])
        row = lax.broadcasted_iota(jnp.int32, shape, 0) + at
        lane = lax.broadcasted_iota(jnp.int32, shape, 1)
        flags = (1 - fin_ref[turn : turn + 1, :]).astype(jnp.float32)
        return jnp.sum(jnp.where(row == lane, flags, 0.0), axis=1, keepdims=True)

    def taken(sl, q, one, two):
        return [
            tap_ref[j, 0:1, sl] * q[j] + tap_ref[j, 1:2, sl] * one[j] + tap_ref[j, 2:3, sl] * two[j]
            for j in range(3)
        ]

    def moving_step(turn):
        if turn > 0:
            @pl.loop(0, chunks[0] // 8)
            def _(i):
                lags = []
                for u in range(8 // CAP):
                    k = lax.rem(dest_ref[turn - 1, i * 8 + u * CAP] - me + groups, groups)
                    lags.append(mrecv[turn - 1][k, 32:48, :].astype(jnp.float32))
                for l in range(2):
                    for j in range(3):
                        at = l * 8 + j * CAP
                        lagn[l, j, pl.ds(pl.multiple_of(i * 8, 8), 8), :] = jnp.concatenate(
                            [lag[at : at + CAP] for lag in lags], axis=0
                        )

        @pl.loop(0, chunks[0] // 16)
        def _(i):
            rows = pl.ds(pl.multiple_of(i * 16, 16), 16)
            mask = alive_column(turn, i * 16) if turn < STEPS - 1 else None

            @pl.loop(0, chans // 128)
            def _(block):
                sl = pl.ds(pl.multiple_of(block * 128, 128), 128)
                lag_ref = lagn if turn > 0 else l_ref
                one = [lag_ref[0, j, rows, sl].astype(jnp.float32) for j in range(3)]
                two = [lag_ref[1, j, rows, sl].astype(jnp.float32) for j in range(3)]
                q = [q_ref[turn, j, rows, sl].astype(jnp.float32) for j in range(3)]
                f = taken(sl, q, one, two)
                xm[rows, sl] = f[0]
                pm[rows, sl] = f[1] * f[2]
                for j in range(3):
                    if turn < STEPS - 1:
                        lagn[0, j, rows, sl] = q[j] * mask
                        lagn[1, j, rows, sl] = one[j] * mask
                    else:
                        lag_out[0, j, rows, sl] = q[j].astype(jnp.bfloat16)
                        lag_out[1, j, rows, sl] = one[j].astype(jnp.bfloat16)

        @pl.loop(0, bands_m)
        def _(b):
            if turn > 0:
                k = lax.rem(dest_ref[turn - 1, b * CAP] - me + groups, groups)
            for r in range(CAP):
                row = b * CAP + r
                for sl in blocks:
                    if turn > 0:
                        s = mrecv[turn - 1][k, 16 * r : 16 * r + 16, sl].astype(jnp.float32)
                    else:
                        s = sm[row, :, sl]
                    s = pole_ref[:, sl] * s + pm[pl.ds(row, 1), sl]
                    ym[pl.ds(row, 1), sl] = jnp.sum(res_ref[:, sl] * s, axis=0, keepdims=True)
                    if turn < STEPS - 1:
                        s = s * alive(turn, row)
                    sm[row, :, sl] = s

        if turn < STEPS - 1:
            @pl.loop(0, chunks[0] // 8)
            def _(i):
                for l in range(2):
                    for j in range(3):
                        at = l * 8 + j * CAP
                        lag = lagn[l, j, pl.ds(pl.multiple_of(i * 8, 8), 8), :]
                        for u in range(8 // CAP):
                            lagm[i * (8 // CAP) + u, at : at + CAP, :] = lag[u * CAP : u * CAP + CAP]

    def moving_gate(turn):
        g_refs[0][turn * chunks[0] : (turn + 1) * chunks[0], :] = (
            xm[...] * (ym[...] + skip_ref[...] * pm[...])
        ).astype(jnp.bfloat16)

    def pack(turn, d, to_ref):
        target = lax.rem(me + d, groups)
        b = lax.fori_loop(
            0,
            bands_m,
            lambda i, found: jnp.where(dest_ref[turn, i * CAP] == target, i, found),
            jnp.int32(0),
        )
        for r in range(CAP):
            to_ref[16 * r : 16 * r + 16, :] = sm[b * CAP + r].astype(jnp.bfloat16)
        to_ref[32:48, :] = lagm[b].astype(jnp.bfloat16)

    def send_moving(turn):
        pack(turn, 0, mrecv[turn].at[0])

        @pl.loop(1, groups)
        def _(d):
            pack(turn, d, msend.at[turn, d])
            migration(turn, d).start()

    def await_moving(turn):
        @pl.loop(1, groups)
        def _(d):
            migration(turn, d).wait_recv()

    def staying(c):
        rows, first, s_ref, g_ref = chunks[c], firsts[c], s_refs[c], g_refs[c]

        @pl.loop(0, rows // 16)
        def _(i):
            at = pl.multiple_of(first + i * 16, 16)
            masks = [alive_column(turn, at) for turn in range(STEPS - 1)]

            @pl.loop(0, chans // 128)
            def _(block):
                sl = pl.ds(pl.multiple_of(block * 128, 128), 128)
                one = [l_ref[0, j, pl.ds(at, 16), sl].astype(jnp.float32) for j in range(3)]
                two = [l_ref[1, j, pl.ds(at, 16), sl].astype(jnp.float32) for j in range(3)]
                for turn in range(STEPS):
                    q = [q_ref[turn, j, pl.ds(at, 16), sl].astype(jnp.float32) for j in range(3)]
                    f = taken(sl, q, one, two)
                    xs[turn, :, sl] = f[0]
                    ps[turn, :, sl] = f[1] * f[2]
                    if turn < STEPS - 1:
                        two = [v * masks[turn] for v in one]
                        one = [v * masks[turn] for v in q]
                    else:
                        for j in range(3):
                            lag_out[0, j, pl.ds(at, 16), sl] = q[j].astype(jnp.bfloat16)
                            lag_out[1, j, pl.ds(at, 16), sl] = one[j].astype(jnp.bfloat16)

            @pl.loop(0, 16)
            def _(r):
                for sl in blocks:
                    s = s_ref[i * 16 + r, :, sl]
                    for turn in range(STEPS):
                        s = pole_ref[:, sl] * s + ps[turn, pl.ds(r, 1), sl]
                        ys[turn, pl.ds(r, 1), sl] = jnp.sum(res_ref[:, sl] * s, axis=0, keepdims=True)
                        if turn < STEPS - 1:
                            s = s * alive(turn, at + r)
                    s_ref[i * 16 + r, :, sl] = s

            for turn in range(STEPS):
                g_ref[pl.ds(pl.multiple_of(turn * rows + i * 16, 16), 16), :] = (
                    xs[turn] * (ys[turn] + skip_ref[...] * ps[turn])
                ).astype(jnp.bfloat16)

    def near_copy(c, s):
        gap = jnp.abs(s - z)
        slot = jnp.where(s > z, 0, 2) + jnp.minimum(gap, 2) - 1
        return pltpu.make_async_remote_copy(
            src_ref=p_refs[c].at[s],
            dst_ref=r_refs[c].at[slot],
            send_sem=rs_sem.at[c, s],
            recv_sem=rr_sem.at[c, slot],
            device_id={"tensor": s},
            device_id_type=MESH,
        )

    def far_copy(c, s):
        return pltpu.make_async_remote_copy(
            src_ref=p_refs[c].at[s],
            dst_ref=relay_refs[c].at[s],
            send_sem=rs_sem.at[c, s],
            recv_sem=rl_sem.at[c, s],
            device_id={"tensor": jnp.where(s > z, z + 1, z - 1)},
            device_id_type=MESH,
        )

    def send_part(c, s):
        gap = jnp.abs(s - z)

        @pl.when(gap <= 2)
        def _():
            near_copy(c, s).start()

        @pl.when(gap > 2)
        def _():
            far_copy(c, s).start()

    def owner_at(i):
        return jnp.where(2 * z < shards, shards - 1 - i, i)

    def relays(s):
        behind = jnp.where(s > z, z > 0, z < shards - 1)
        return jnp.logical_and(jnp.abs(s - z) >= 2, behind)

    def product(c, s):
        return jnp.dot(
            g_refs[c][...],
            w_ref[:, pl.ds(pl.multiple_of(s * cols, cols), cols)],
            preferred_element_type=jnp.float32,
        )

    def project(c):
        @pl.loop(0, shards)
        def _(i):
            s = owner_at(i)

            @pl.when(jnp.logical_and(s != z, jnp.logical_not(relays(s))))
            def _():
                p_refs[c][s] = product(c, s).astype(jnp.bfloat16)
                send_part(c, s)

        t_refs[c][...] = product(c, z)

    def relay(c):
        @pl.loop(0, shards)
        def _(i):
            s = owner_at(i)

            @pl.when(jnp.logical_and(s != z, relays(s)))
            def _():
                part = product(c, s)
                far_copy(c, s).wait_recv()
                p_refs[c][s] = (part + relay_refs[c][s].astype(jnp.float32)).astype(jnp.bfloat16)
                send_part(c, s)

    here = [z >= 1, z >= 2, z <= shards - 2, z <= shards - 3]

    def pieces(rows):
        return [(i, min(128, rows - i)) for i in range(0, rows, 128)]

    def eye(size):
        return lax.broadcasted_iota(jnp.int32, (size, 128), 0) == lax.broadcasted_iota(
            jnp.int32, (size, 128), 1
        )

    def square_copy(c, j):
        return pltpu.make_async_remote_copy(
            src_ref=ss_own.at[c],
            dst_ref=ss_recv.at[c, j],
            send_sem=ss_sem.at[c, j],
            recv_sem=sr_sem.at[c, j],
            device_id={"tensor": lax.rem(z + j, shards)},
            device_id_type=MESH,
        )

    def collect(c):
        r_ref, t_ref = r_refs[c], t_refs[c]
        for slot in range(4):
            @pl.when(here[slot])
            def _():
                pltpu.make_async_remote_copy(
                    src_ref=r_ref.at[slot],
                    dst_ref=r_ref.at[slot],
                    send_sem=rs_sem.at[c, 0],
                    recv_sem=rr_sem.at[c, slot],
                    device_id={"tensor": lax.rem(z + 1, shards)},
                    device_id_type=MESH,
                ).wait_recv()
                t_ref[...] += r_ref[slot].astype(jnp.float32)

        for at, (i, size) in enumerate(pieces(t_ref.shape[0])):
            x = t_ref[i : i + size, :]
            squares = jnp.sum(x * x, axis=1, keepdims=True)
            ss_own[c, at : at + 1, :] = jnp.sum(
                jnp.where(eye(size), squares, 0.0), axis=0, keepdims=True
            )
        for j in range(1, shards):
            square_copy(c, j).start()

    def finish(c):
        t_ref, rows, first = t_refs[c], chunks[c], firsts[c]
        for j in range(1, shards):
            square_copy(c, j).wait_recv()
        total = ss_own[c]
        for j in range(1, shards):
            total = total + ss_recv[c, j]
        for at, (i, size) in enumerate(pieces(t_ref.shape[0])):
            squares = jnp.sum(jnp.where(eye(size), total[at : at + 1], 0.0), axis=1, keepdims=True)
            scale = lax.rsqrt(squares / (cols * shards) + 1e-05)
            value = (t_ref[i : i + size, :] * scale * gain_ref[...]).astype(jnp.bfloat16)
            for turn in range(i // rows, (i + size) // rows):
                part = turn * rows - i
                mix_out[turn, first : first + rows, :] = value[part : part + rows]

    def stay(c):
        loads[c].wait()
        staying(c)
        stores[c].start()
        if c == 1:
            load_w.wait()
        project(c)

    loads[0].wait()
    moving_step(0)
    pl.semaphore_wait(barrier, groups + shards - 2)
    send_moving(0)
    moving_gate(0)
    stay(1)
    await_moving(0)
    moving_step(1)
    send_moving(1)
    moving_gate(1)
    relay(1)
    for c in range(2, nc):
        stay(c)
    await_moving(1)
    moving_step(2)
    send_moving(2)
    moving_gate(2)
    for c in range(2, nc):
        relay(c)
    await_moving(2)
    moving_step(3)
    moving_gate(3)
    stores[0].start()
    project(0)
    collect(1)
    relay(0)
    for c in range(2, nc):
        collect(c)
    for c in range(1, nc):
        finish(c)
    collect(0)
    finish(0)
    for turn in range(STEPS - 1):
        @pl.loop(1, groups)
        def _(d):
            migration(turn, d).wait_send()
    for c in range(nc):
        @pl.loop(0, shards)
        def _(s):
            @pl.when(s != z)
            def _():
                near_copy(c, s).wait_send()

        for j in range(1, shards):
            square_copy(c, j).wait_send()
    for store in stores:
        store.wait()


def per_device(
    qkv,
    fir_buffer,
    fir_taps,
    modal_state,
    poles,
    residues,
    skip,
    out_weight,
    norm_gain,
    finished,
    dest_group,
):
    groups = lax.axis_size("dp")
    shards = lax.axis_size("tensor")
    rows, order, chans = modal_state.shape
    cols = norm_gain.shape[0]
    f32 = jnp.float32
    bf16 = jnp.bfloat16

    moving = groups * CAP
    left = rows - moving
    half = left // 32 * 16
    chunks = (moving,) + ((half, left - half) if half else (left,))
    nc = len(chunks)
    tall = [STEPS * n for n in chunks]
    vmem = pl.BlockSpec(memory_space=pltpu.VMEM)
    smem = pl.BlockSpec(memory_space=pltpu.SMEM)
    hbm = pl.BlockSpec(memory_space=pl.ANY)
    dma = pltpu.SemaphoreType.DMA
    outs = pl.pallas_call(
        functools.partial(kernel, groups, shards, chunks),
        out_shape=[
            jax.ShapeDtypeStruct((STEPS, rows, cols), bf16),
            jax.ShapeDtypeStruct(modal_state.shape, f32),
            jax.ShapeDtypeStruct((2, 3, rows, chans), bf16),
        ],
        in_specs=[vmem] * 4 + [hbm, vmem, vmem, vmem, hbm, vmem, smem, smem],
        out_specs=[vmem, hbm, vmem],
        scratch_shapes=[pltpu.VMEM((n, order, chans), f32) for n in chunks]
        + [
            pltpu.VMEM(out_weight.shape, bf16),
            pltpu.VMEM((2, 3, moving, chans), f32),
            pltpu.VMEM((groups, 16, chans), f32),
            pltpu.VMEM((STEPS - 1, groups, 48, chans), bf16),
        ]
        + [pltpu.VMEM((groups, 48, chans), bf16)] * (STEPS - 1)
        + [pltpu.VMEM((moving, chans), f32)] * 3
        + [pltpu.VMEM((STEPS, 16, chans), f32)] * 3
        + [pltpu.VMEM((n, chans), bf16) for n in tall]
        + [pltpu.VMEM((shards, n, cols), bf16) for n in tall]
        + [pltpu.VMEM((4, n, cols), bf16) for n in tall]
        + [pltpu.VMEM((shards, n, cols), bf16) for n in tall]
        + [pltpu.VMEM((n, cols), f32) for n in tall]
        + [
            pltpu.VMEM((nc, 8, 128), f32),
            pltpu.VMEM((nc, shards, 8, 128), f32),
            dma((nc + 1,)),
            dma((nc,)),
            dma((STEPS - 1, groups)),
            dma((STEPS - 1, groups)),
            dma((nc, shards)),
            dma((nc, 4)),
            dma((nc, shards)),
            dma((nc, shards)),
            dma((nc, shards)),
        ],
        compiler_params=pltpu.CompilerParams(
            collective_id=0, has_side_effects=True, vmem_limit_bytes=56 * 1024 * 1024
        ),
        name="mixer",
    )(
        qkv.transpose(0, 2, 1, 3),
        fir_buffer.transpose(2, 1, 0, 3),
        fir_taps,
        finished,
        modal_state,
        poles,
        residues,
        skip[None],
        out_weight,
        norm_gain[None],
        finished,
        dest_group,
    )
    mixed, state, lagged = outs
    return (mixed, state, lagged.transpose(2, 1, 0, 3))


def solution(mesh):
    return jax.shard_map(
        per_device,
        mesh=mesh,
        in_specs=(
            P(None, "dp", None, "tensor"),
            P("dp", None, None, "tensor"),
            P(None, None, "tensor"),
            P("dp", None, "tensor"),
            P(None, "tensor"),
            P(None, "tensor"),
            P("tensor"),
            P("tensor", None),
            P("tensor"),
            P(None, "dp"),
            P(None, "dp"),
        ),
        out_specs=(P(None, "dp", "tensor"), P("dp", None, "tensor"), P("dp", None, None, "tensor")),
        check_vma=False,
    )
```

```python
import functools

import jax
import jax.numpy as jnp
from jax import lax
from jax.experimental import pallas as pl
from jax.experimental.pallas import tpu as pltpu
from jax.sharding import PartitionSpec as P

STEPS = 4
CAP = 2
MESH = pl.DeviceIdType.MESH
LANES = 512


def row_update(poles, res, skip, s, x, p):
    s = poles * s + p
    y = jnp.sum(res * s, axis=0, keepdims=True) + skip * p
    return s, x * y


def kernel(groups, shards, chunks, *refs):
    refs = list(refs)

    def take(count):
        got = refs[:count]
        del refs[:count]
        return got

    nc = len(chunks)
    q_ref, l_ref, tap_ref, fin_ref = take(4)
    st_ref, pole_ref, res_ref, skip_ref, w_hbm, gain_ref = take(6)
    done_ref, dest_ref = take(2)
    mix_out, st_out, lag_out = take(3)
    s_refs = take(nc)
    w_ref, lagn, lagm, msend = take(4)
    mrecv = take(STEPS - 1)
    xm, pm, ym, xs, ps, ys = take(6)
    g_refs, p_refs, r_refs, relay_refs, t_refs = take(nc), take(nc), take(nc), take(nc), take(nc)
    ss_own, ss_recv = take(2)
    load_sem, store_sem, ms_sem, mr_sem, rs_sem, rr_sem, rl_sem, ss_sem, sr_sem = take(9)
    sm = s_refs[0]
    me = lax.axis_index("dp")
    z = lax.axis_index("tensor")
    cols = gain_ref.shape[1]
    chans = pole_ref.shape[1]
    lanes = min(LANES, chans)
    blocks = [slice(i, i + lanes) for i in range(0, chans, lanes)]
    bands_m = chunks[0] // CAP
    firsts = [sum(chunks[:c]) for c in range(nc)]

    barrier = pltpu.get_barrier_semaphore()

    @pl.loop(1, groups)
    def _(d):
        pl.semaphore_signal(barrier, inc=1, device_id={"dp": lax.rem(me + d, groups)}, device_id_type=MESH)

    @pl.loop(1, shards)
    def _(d):
        pl.semaphore_signal(barrier, inc=1, device_id={"tensor": lax.rem(z + d, shards)}, device_id_type=MESH)

    loads = [
        pltpu.make_async_copy(st_ref.at[pl.ds(firsts[c], chunks[c])], s_refs[c], load_sem.at[c])
        for c in range(nc)
    ]
    load_w = pltpu.make_async_copy(w_hbm, w_ref, load_sem.at[nc])
    stores = [
        pltpu.make_async_copy(s_refs[c], st_out.at[pl.ds(firsts[c], chunks[c])], store_sem.at[c])
        for c in range(nc)
    ]
    loads[0].start()
    loads[1].start()
    load_w.start()
    for load in loads[2:]:
        load.start()
    ss_own[...] = jnp.zeros_like(ss_own)
    lagm[...] = jnp.zeros_like(lagm)

    def migration(turn, d):
        return pltpu.make_async_remote_copy(
            src_ref=msend.at[turn, d],
            dst_ref=mrecv[turn].at[d],
            send_sem=ms_sem.at[turn, d],
            recv_sem=mr_sem.at[turn, d],
            device_id={"dp": lax.rem(me + d, groups)},
            device_id_type=MESH,
        )

    def alive(turn, row):
        return (1 - done_ref[turn, row]).astype(jnp.float32)

    def alive_column(turn, at):
        shape = (16, fin_ref.shape[1])
        row = lax.broadcasted_iota(jnp.int32, shape, 0) + at
        lane = lax.broadcasted_iota(jnp.int32, shape, 1)
        flags = (1 - fin_ref[turn : turn + 1, :]).astype(jnp.float32)
        return jnp.sum(jnp.where(row == lane, flags, 0.0), axis=1, keepdims=True)

    def taken(sl, q, one, two):
        return [
            tap_ref[j, 0:1, sl] * q[j] + tap_ref[j, 1:2, sl] * one[j] + tap_ref[j, 2:3, sl] * two[j]
            for j in range(3)
        ]

    def moving_step(turn):
        if turn > 0:
            @pl.loop(0, chunks[0] // 8)
            def _(i):
                lags = []
                for u in range(8 // CAP):
                    k = lax.rem(dest_ref[turn - 1, i * 8 + u * CAP] - me + groups, groups)
                    lags.append(mrecv[turn - 1][k, 32:48, :].astype(jnp.float32))
                for l in range(2):
                    for j in range(3):
                        at = l * 8 + j * CAP
                        lagn[l, j, pl.ds(pl.multiple_of(i * 8, 8), 8), :] = jnp.concatenate(
                            [lag[at : at + CAP] for lag in lags], axis=0
                        )

        @pl.loop(0, chunks[0] // 16)
        def _(i):
            rows = pl.ds(pl.multiple_of(i * 16, 16), 16)
            mask = alive_column(turn, i * 16) if turn < STEPS - 1 else None

            @pl.loop(0, chans // 128)
            def _(block):
                sl = pl.ds(pl.multiple_of(block * 128, 128), 128)
                lag_ref = lagn if turn > 0 else l_ref
                one = [lag_ref[0, j, rows, sl].astype(jnp.float32) for j in range(3)]
                two = [lag_ref[1, j, rows, sl].astype(jnp.float32) for j in range(3)]
                q = [q_ref[turn, j, rows, sl].astype(jnp.float32) for j in range(3)]
                f = taken(sl, q, one, two)
                xm[rows, sl] = f[0]
                pm[rows, sl] = f[1] * f[2]
                for j in range(3):
                    if turn < STEPS - 1:
                        lagn[0, j, rows, sl] = q[j] * mask
                        lagn[1, j, rows, sl] = one[j] * mask
                    else:
                        lag_out[0, j, rows, sl] = q[j].astype(jnp.bfloat16)
                        lag_out[1, j, rows, sl] = one[j].astype(jnp.bfloat16)

        @pl.loop(0, bands_m)
        def _(b):
            if turn > 0:
                k = lax.rem(dest_ref[turn - 1, b * CAP] - me + groups, groups)
            for r in range(CAP):
                row = b * CAP + r
                for sl in blocks:
                    if turn > 0:
                        s = mrecv[turn - 1][k, 16 * r : 16 * r + 16, sl].astype(jnp.float32)
                    else:
                        s = sm[row, :, sl]
                    s = pole_ref[:, sl] * s + pm[pl.ds(row, 1), sl]
                    ym[pl.ds(row, 1), sl] = jnp.sum(res_ref[:, sl] * s, axis=0, keepdims=True)
                    if turn < STEPS - 1:
                        s = s * alive(turn, row)
                    sm[row, :, sl] = s

        if turn < STEPS - 1:
            @pl.loop(0, chunks[0] // 8)
            def _(i):
                for l in range(2):
                    for j in range(3):
                        at = l * 8 + j * CAP
                        lag = lagn[l, j, pl.ds(pl.multiple_of(i * 8, 8), 8), :]
                        for u in range(8 // CAP):
                            lagm[i * (8 // CAP) + u, at : at + CAP, :] = lag[u * CAP : u * CAP + CAP]

    def moving_gate(turn):
        g_refs[0][turn * chunks[0] : (turn + 1) * chunks[0], :] = (
            xm[...] * (ym[...] + skip_ref[...] * pm[...])
        ).astype(jnp.bfloat16)

    def pack(turn, d, to_ref):
        target = lax.rem(me + d, groups)
        b = lax.fori_loop(
            0,
            bands_m,
            lambda i, found: jnp.where(dest_ref[turn, i * CAP] == target, i, found),
            jnp.int32(0),
        )
        for r in range(CAP):
            to_ref[16 * r : 16 * r + 16, :] = sm[b * CAP + r].astype(jnp.bfloat16)
        to_ref[32:48, :] = lagm[b].astype(jnp.bfloat16)

    def send_moving(turn):
        pack(turn, 0, mrecv[turn].at[0])

        @pl.loop(1, groups)
        def _(d):
            pack(turn, d, msend.at[turn, d])
            migration(turn, d).start()

    def await_moving(turn):
        @pl.loop(1, groups)
        def _(d):
            migration(turn, d).wait_recv()

    def staying(c):
        rows, first, s_ref, g_ref = chunks[c], firsts[c], s_refs[c], g_refs[c]

        @pl.loop(0, rows // 16)
        def _(i):
            at = pl.multiple_of(first + i * 16, 16)
            masks = [alive_column(turn, at) for turn in range(STEPS - 1)]

            @pl.loop(0, chans // 128)
            def _(block):
                sl = pl.ds(pl.multiple_of(block * 128, 128), 128)
                one = [l_ref[0, j, pl.ds(at, 16), sl].astype(jnp.float32) for j in range(3)]
                two = [l_ref[1, j, pl.ds(at, 16), sl].astype(jnp.float32) for j in range(3)]
                for turn in range(STEPS):
                    q = [q_ref[turn, j, pl.ds(at, 16), sl].astype(jnp.float32) for j in range(3)]
                    f = taken(sl, q, one, two)
                    xs[turn, :, sl] = f[0]
                    ps[turn, :, sl] = f[1] * f[2]
                    if turn < STEPS - 1:
                        two = [v * masks[turn] for v in one]
                        one = [v * masks[turn] for v in q]
                    else:
                        for j in range(3):
                            lag_out[0, j, pl.ds(at, 16), sl] = q[j].astype(jnp.bfloat16)
                            lag_out[1, j, pl.ds(at, 16), sl] = one[j].astype(jnp.bfloat16)

            @pl.loop(0, 16)
            def _(r):
                for sl in blocks:
                    s = s_ref[i * 16 + r, :, sl]
                    for turn in range(STEPS):
                        s = pole_ref[:, sl] * s + ps[turn, pl.ds(r, 1), sl]
                        ys[turn, pl.ds(r, 1), sl] = jnp.sum(res_ref[:, sl] * s, axis=0, keepdims=True)
                        if turn < STEPS - 1:
                            s = s * alive(turn, at + r)
                    s_ref[i * 16 + r, :, sl] = s

            for turn in range(STEPS):
                g_ref[pl.ds(pl.multiple_of(turn * rows + i * 16, 16), 16), :] = (
                    xs[turn] * (ys[turn] + skip_ref[...] * ps[turn])
                ).astype(jnp.bfloat16)

    def near_copy(c, s):
        gap = jnp.abs(s - z)
        slot = jnp.where(s > z, 0, 2) + jnp.minimum(gap, 2) - 1
        return pltpu.make_async_remote_copy(
            src_ref=p_refs[c].at[s],
            dst_ref=r_refs[c].at[slot],
            send_sem=rs_sem.at[c, s],
            recv_sem=rr_sem.at[c, slot],
            device_id={"tensor": s},
            device_id_type=MESH,
        )

    def far_copy(c, s):
        return pltpu.make_async_remote_copy(
            src_ref=p_refs[c].at[s],
            dst_ref=relay_refs[c].at[s],
            send_sem=rs_sem.at[c, s],
            recv_sem=rl_sem.at[c, s],
            device_id={"tensor": jnp.where(s > z, z + 1, z - 1)},
            device_id_type=MESH,
        )

    def send_part(c, s):
        gap = jnp.abs(s - z)

        @pl.when(gap <= 2)
        def _():
            near_copy(c, s).start()

        @pl.when(gap > 2)
        def _():
            far_copy(c, s).start()

    def owner_at(i):
        return jnp.where(2 * z < shards, shards - 1 - i, i)

    def relays(s):
        behind = jnp.where(s > z, z > 0, z < shards - 1)
        return jnp.logical_and(jnp.abs(s - z) >= 2, behind)

    def product(c, s):
        return jnp.dot(
            g_refs[c][...],
            w_ref[:, pl.ds(pl.multiple_of(s * cols, cols), cols)],
            preferred_element_type=jnp.float32,
        )

    def project(c):
        @pl.loop(0, shards)
        def _(i):
            s = owner_at(i)

            @pl.when(jnp.logical_and(s != z, jnp.logical_not(relays(s))))
            def _():
                p_refs[c][s] = product(c, s).astype(jnp.bfloat16)
                send_part(c, s)

        t_refs[c][...] = product(c, z)

    def relay(c):
        @pl.loop(0, shards)
        def _(i):
            s = owner_at(i)

            @pl.when(jnp.logical_and(s != z, relays(s)))
            def _():
                part = product(c, s)
                far_copy(c, s).wait_recv()
                p_refs[c][s] = (part + relay_refs[c][s].astype(jnp.float32)).astype(jnp.bfloat16)
                send_part(c, s)

    here = [z >= 1, z >= 2, z <= shards - 2, z <= shards - 3]

    def pieces(rows):
        return [(i, min(128, rows - i)) for i in range(0, rows, 128)]

    def eye(size):
        return lax.broadcasted_iota(jnp.int32, (size, 128), 0) == lax.broadcasted_iota(
            jnp.int32, (size, 128), 1
        )

    def square_copy(c, j):
        return pltpu.make_async_remote_copy(
            src_ref=ss_own.at[c],
            dst_ref=ss_recv.at[c, j],
            send_sem=ss_sem.at[c, j],
            recv_sem=sr_sem.at[c, j],
            device_id={"tensor": lax.rem(z + j, shards)},
            device_id_type=MESH,
        )

    def collect(c):
        r_ref, t_ref = r_refs[c], t_refs[c]
        for slot in range(4):
            @pl.when(here[slot])
            def _():
                pltpu.make_async_remote_copy(
                    src_ref=r_ref.at[slot],
                    dst_ref=r_ref.at[slot],
                    send_sem=rs_sem.at[c, 0],
                    recv_sem=rr_sem.at[c, slot],
                    device_id={"tensor": lax.rem(z + 1, shards)},
                    device_id_type=MESH,
                ).wait_recv()
                t_ref[...] += r_ref[slot].astype(jnp.float32)

        for at, (i, size) in enumerate(pieces(t_ref.shape[0])):
            x = t_ref[i : i + size, :]
            squares = jnp.sum(x * x, axis=1, keepdims=True)
            ss_own[c, at : at + 1, :] = jnp.sum(
                jnp.where(eye(size), squares, 0.0), axis=0, keepdims=True
            )
        for j in range(1, shards):
            square_copy(c, j).start()

    def finish(c):
        t_ref, rows, first = t_refs[c], chunks[c], firsts[c]
        for j in range(1, shards):
            square_copy(c, j).wait_recv()
        total = ss_own[c]
        for j in range(1, shards):
            total = total + ss_recv[c, j]
        for at, (i, size) in enumerate(pieces(t_ref.shape[0])):
            squares = jnp.sum(jnp.where(eye(size), total[at : at + 1], 0.0), axis=1, keepdims=True)
            scale = lax.rsqrt(squares / (cols * shards) + 1e-05)
            value = (t_ref[i : i + size, :] * scale * gain_ref[...]).astype(jnp.bfloat16)
            for turn in range(i // rows, (i + size) // rows):
                part = turn * rows - i
                mix_out[turn, first : first + rows, :] = value[part : part + rows]

    def stay(c):
        loads[c].wait()
        staying(c)
        stores[c].start()
        if c == 1:
            load_w.wait()
        project(c)

    loads[0].wait()
    moving_step(0)
    pl.semaphore_wait(barrier, groups + shards - 2)
    send_moving(0)
    moving_gate(0)
    stay(1)
    await_moving(0)
    moving_step(1)
    send_moving(1)
    moving_gate(1)
    relay(1)
    for c in range(2, nc):
        stay(c)
    await_moving(1)
    moving_step(2)
    send_moving(2)
    moving_gate(2)
    for c in range(2, nc):
        relay(c)
    await_moving(2)
    moving_step(3)
    moving_gate(3)
    stores[0].start()
    project(0)
    collect(1)
    relay(0)
    for c in range(2, nc):
        collect(c)
    for c in range(1, nc):
        finish(c)
    collect(0)
    finish(0)
    for turn in range(STEPS - 1):
        @pl.loop(1, groups)
        def _(d):
            migration(turn, d).wait_send()
    for c in range(nc):
        @pl.loop(0, shards)
        def _(s):
            @pl.when(s != z)
            def _():
                near_copy(c, s).wait_send()

        for j in range(1, shards):
            square_copy(c, j).wait_send()
    for store in stores:
        store.wait()


def per_device(
    qkv,
    fir_buffer,
    fir_taps,
    modal_state,
    poles,
    residues,
    skip,
    out_weight,
    norm_gain,
    finished,
    dest_group,
):
    groups = lax.axis_size("dp")
    shards = lax.axis_size("tensor")
    rows, order, chans = modal_state.shape
    cols = norm_gain.shape[0]
    f32 = jnp.float32
    bf16 = jnp.bfloat16

    moving = groups * CAP
    left = rows - moving
    half = left // 32 * 16
    chunks = (moving,) + ((half, left - half) if half else (left,))
    nc = len(chunks)
    tall = [STEPS * n for n in chunks]
    vmem = pl.BlockSpec(memory_space=pltpu.VMEM)
    smem = pl.BlockSpec(memory_space=pltpu.SMEM)
    hbm = pl.BlockSpec(memory_space=pl.ANY)
    dma = pltpu.SemaphoreType.DMA
    outs = pl.pallas_call(
        functools.partial(kernel, groups, shards, chunks),
        out_shape=[
            jax.ShapeDtypeStruct((STEPS, rows, cols), bf16),
            jax.ShapeDtypeStruct(modal_state.shape, f32),
            jax.ShapeDtypeStruct((2, 3, rows, chans), bf16),
        ],
        in_specs=[vmem] * 4 + [hbm, vmem, vmem, vmem, hbm, vmem, smem, smem],
        out_specs=[vmem, hbm, vmem],
        scratch_shapes=[pltpu.VMEM((n, order, chans), f32) for n in chunks]
        + [
            pltpu.VMEM(out_weight.shape, bf16),
            pltpu.VMEM((2, 3, moving, chans), f32),
            pltpu.VMEM((groups, 16, chans), f32),
            pltpu.VMEM((STEPS - 1, groups, 48, chans), bf16),
        ]
        + [pltpu.VMEM((groups, 48, chans), bf16)] * (STEPS - 1)
        + [pltpu.VMEM((moving, chans), f32)] * 3
        + [pltpu.VMEM((STEPS, 16, chans), f32)] * 3
        + [pltpu.VMEM((n, chans), bf16) for n in tall]
        + [pltpu.VMEM((shards, n, cols), bf16) for n in tall]
        + [pltpu.VMEM((4, n, cols), bf16) for n in tall]
        + [pltpu.VMEM((shards, n, cols), bf16) for n in tall]
        + [pltpu.VMEM((n, cols), f32) for n in tall]
        + [
            pltpu.VMEM((nc, 8, 128), f32),
            pltpu.VMEM((nc, shards, 8, 128), f32),
            dma((nc + 1,)),
            dma((nc,)),
            dma((STEPS - 1, groups)),
            dma((STEPS - 1, groups)),
            dma((nc, shards)),
            dma((nc, 4)),
            dma((nc, shards)),
            dma((nc, shards)),
            dma((nc, shards)),
        ],
        compiler_params=pltpu.CompilerParams(
            collective_id=0, has_side_effects=True, vmem_limit_bytes=38 * 1024 * 1024
        ),
        name="mixer",
    )(
        qkv.transpose(0, 2, 1, 3),
        fir_buffer.transpose(2, 1, 0, 3),
        fir_taps,
        finished,
        modal_state,
        poles,
        residues,
        skip[None],
        out_weight,
        norm_gain[None],
        finished,
        dest_group,
    )
    mixed, state, lagged = outs
    return (mixed, state, lagged.transpose(2, 1, 0, 3))


def solution(mesh):
    return jax.shard_map(
        per_device,
        mesh=mesh,
        in_specs=(
            P(None, "dp", None, "tensor"),
            P("dp", None, None, "tensor"),
            P(None, None, "tensor"),
            P("dp", None, "tensor"),
            P(None, "tensor"),
            P(None, "tensor"),
            P("tensor"),
            P("tensor", None),
            P("tensor"),
            P(None, "dp"),
            P(None, "dp"),
        ),
        out_specs=(P(None, "dp", "tensor"), P("dp", None, "tensor"), P("dp", None, None, "tensor")),
        check_vma=False,
    )
```

```python
import functools

import jax
import jax.numpy as jnp
from jax import lax
from jax.experimental import pallas as pl
from jax.experimental.pallas import tpu as pltpu
from jax.sharding import PartitionSpec as P

STEPS = 4
CAP = 2
MESH = pl.DeviceIdType.MESH
LANES = 512


def row_update(poles, res, skip, s, x, p):
    s = poles * s + p
    y = jnp.sum(res * s, axis=0, keepdims=True) + skip * p
    return s, x * y


def kernel(groups, shards, chunks, *refs):
    refs = list(refs)

    def take(count):
        got = refs[:count]
        del refs[:count]
        return got

    nc = len(chunks)
    l_ref, fin_ref, st_ref, w_hbm = take(4)
    small_hbm = take(6)
    done_ref, dest_ref = take(2)
    mix_out, st_out, lag_out = take(3)
    s_refs = take(nc)
    small_refs = take(6)
    q_ref, tap_ref, pole_ref, res_ref, skip_ref, gain_ref = small_refs
    w_ref, lagn, lagm, msend = take(4)
    mrecv = take(STEPS - 1)
    xm, pm, ym, xs, ps, ys = take(6)
    np = nc + 1
    g_refs, p_refs, r_refs, relay_refs, t_refs = take(np), take(np), take(np), take(np), take(np)
    ss_own, ss_recv = take(2)
    load_sem, store_sem, ms_sem, mr_sem, rs_sem, rr_sem, rl_sem, ss_sem, sr_sem = take(9)
    sm = s_refs[0]
    me = lax.axis_index("dp")
    z = lax.axis_index("tensor")
    cols = gain_ref.shape[1]
    chans = pole_ref.shape[1]
    lanes = min(LANES, chans)
    blocks = [slice(i, i + lanes) for i in range(0, chans, lanes)]
    bands_m = chunks[0] // CAP
    firsts = [sum(chunks[:c]) for c in range(nc)]

    barrier = pltpu.get_barrier_semaphore()

    @pl.loop(1, groups)
    def _(d):
        pl.semaphore_signal(barrier, inc=1, device_id={"dp": lax.rem(me + d, groups)}, device_id_type=MESH)

    @pl.loop(1, shards)
    def _(d):
        pl.semaphore_signal(barrier, inc=1, device_id={"tensor": lax.rem(z + d, shards)}, device_id_type=MESH)

    loads = [
        pltpu.make_async_copy(st_ref.at[pl.ds(firsts[c], chunks[c])], s_refs[c], load_sem.at[c])
        for c in range(nc)
    ]
    load_w = pltpu.make_async_copy(w_hbm, w_ref, load_sem.at[nc])
    stores = [
        pltpu.make_async_copy(s_refs[c], st_out.at[pl.ds(firsts[c], chunks[c])], store_sem.at[c])
        for c in range(nc)
    ]
    small_loads = [
        pltpu.make_async_copy(small_hbm[i], small_refs[i], load_sem.at[nc + 1 + i]) for i in range(6)
    ]
    for load in small_loads:
        load.start()
    loads[0].start()
    loads[1].start()
    load_w.start()
    for load in loads[2:]:
        load.start()
    ss_own[...] = jnp.zeros_like(ss_own)
    lagm[...] = jnp.zeros_like(lagm)

    def migration(turn, d):
        return pltpu.make_async_remote_copy(
            src_ref=msend.at[turn, d],
            dst_ref=mrecv[turn].at[d],
            send_sem=ms_sem.at[turn, d],
            recv_sem=mr_sem.at[turn, d],
            device_id={"dp": lax.rem(me + d, groups)},
            device_id_type=MESH,
        )

    def alive(turn, row):
        return (1 - done_ref[turn, row]).astype(jnp.float32)

    def alive_column(turn, at):
        shape = (16, fin_ref.shape[1])
        row = lax.broadcasted_iota(jnp.int32, shape, 0) + at
        lane = lax.broadcasted_iota(jnp.int32, shape, 1)
        flags = (1 - fin_ref[turn : turn + 1, :]).astype(jnp.float32)
        return jnp.sum(jnp.where(row == lane, flags, 0.0), axis=1, keepdims=True)

    def taken(sl, q, one, two):
        return [
            tap_ref[j, 0:1, sl] * q[j] + tap_ref[j, 1:2, sl] * one[j] + tap_ref[j, 2:3, sl] * two[j]
            for j in range(3)
        ]

    def moving_step(turn):
        if turn > 0:
            @pl.loop(0, chunks[0] // 8)
            def _(i):
                lags = []
                for u in range(8 // CAP):
                    k = lax.rem(dest_ref[turn - 1, i * 8 + u * CAP] - me + groups, groups)
                    lags.append(mrecv[turn - 1][k, 32:48, :].astype(jnp.float32))
                for l in range(2):
                    for j in range(3):
                        at = l * 8 + j * CAP
                        lagn[l, j, pl.ds(pl.multiple_of(i * 8, 8), 8), :] = jnp.concatenate(
                            [lag[at : at + CAP] for lag in lags], axis=0
                        )

        @pl.loop(0, chunks[0] // 16)
        def _(i):
            rows = pl.ds(pl.multiple_of(i * 16, 16), 16)
            mask = alive_column(turn, i * 16) if turn < STEPS - 1 else None

            @pl.loop(0, chans // 128)
            def _(block):
                sl = pl.ds(pl.multiple_of(block * 128, 128), 128)
                lag_ref = lagn if turn > 0 else l_ref
                one = [lag_ref[0, j, rows, sl].astype(jnp.float32) for j in range(3)]
                two = [lag_ref[1, j, rows, sl].astype(jnp.float32) for j in range(3)]
                q = [q_ref[turn, j, rows, sl].astype(jnp.float32) for j in range(3)]
                f = taken(sl, q, one, two)
                xm[rows, sl] = f[0]
                pm[rows, sl] = f[1] * f[2]
                for j in range(3):
                    if turn < STEPS - 1:
                        lagn[0, j, rows, sl] = q[j] * mask
                        lagn[1, j, rows, sl] = one[j] * mask
                    else:
                        lag_out[0, j, rows, sl] = q[j].astype(jnp.bfloat16)
                        lag_out[1, j, rows, sl] = one[j].astype(jnp.bfloat16)

        @pl.loop(0, bands_m)
        def _(b):
            if turn > 0:
                k = lax.rem(dest_ref[turn - 1, b * CAP] - me + groups, groups)
            for r in range(CAP):
                row = b * CAP + r
                for sl in blocks:
                    if turn > 0:
                        s = mrecv[turn - 1][k, 16 * r : 16 * r + 16, sl].astype(jnp.float32)
                    else:
                        s = sm[row, :, sl]
                    s = pole_ref[:, sl] * s + pm[pl.ds(row, 1), sl]
                    ym[pl.ds(row, 1), sl] = jnp.sum(res_ref[:, sl] * s, axis=0, keepdims=True)
                    if turn < STEPS - 1:
                        s = s * alive(turn, row)
                    sm[row, :, sl] = s

        if turn < STEPS - 1:
            @pl.loop(0, chunks[0] // 8)
            def _(i):
                for l in range(2):
                    for j in range(3):
                        at = l * 8 + j * CAP
                        lag = lagn[l, j, pl.ds(pl.multiple_of(i * 8, 8), 8), :]
                        for u in range(8 // CAP):
                            lagm[i * (8 // CAP) + u, at : at + CAP, :] = lag[u * CAP : u * CAP + CAP]

    def moving_gate(turn):
        g_ref, at = (g_refs[nc], turn * chunks[0]) if turn < STEPS - 1 else (g_refs[0], 0)
        g_ref[at : at + chunks[0], :] = (
            xm[...] * (ym[...] + skip_ref[...] * pm[...])
        ).astype(jnp.bfloat16)

    def pack(turn, d, to_ref):
        target = lax.rem(me + d, groups)
        b = lax.fori_loop(
            0,
            bands_m,
            lambda i, found: jnp.where(dest_ref[turn, i * CAP] == target, i, found),
            jnp.int32(0),
        )
        for r in range(CAP):
            to_ref[16 * r : 16 * r + 16, :] = sm[b * CAP + r].astype(jnp.bfloat16)
        to_ref[32:48, :] = lagm[b].astype(jnp.bfloat16)

    def send_moving(turn):
        pack(turn, 0, mrecv[turn].at[0])

        @pl.loop(1, groups)
        def _(d):
            pack(turn, d, msend.at[turn, d])
            migration(turn, d).start()

    def await_moving(turn):
        @pl.loop(1, groups)
        def _(d):
            migration(turn, d).wait_recv()

    def staying(c):
        rows, first, s_ref, g_ref = chunks[c], firsts[c], s_refs[c], g_refs[c]

        @pl.loop(0, rows // 16)
        def _(i):
            at = pl.multiple_of(first + i * 16, 16)
            masks = [alive_column(turn, at) for turn in range(STEPS - 1)]

            @pl.loop(0, chans // 128)
            def _(block):
                sl = pl.ds(pl.multiple_of(block * 128, 128), 128)
                one = [l_ref[0, j, pl.ds(at, 16), sl].astype(jnp.float32) for j in range(3)]
                two = [l_ref[1, j, pl.ds(at, 16), sl].astype(jnp.float32) for j in range(3)]
                for turn in range(STEPS):
                    q = [q_ref[turn, j, pl.ds(at, 16), sl].astype(jnp.float32) for j in range(3)]
                    f = taken(sl, q, one, two)
                    xs[turn, :, sl] = f[0]
                    ps[turn, :, sl] = f[1] * f[2]
                    if turn < STEPS - 1:
                        two = [v * masks[turn] for v in one]
                        one = [v * masks[turn] for v in q]
                    else:
                        for j in range(3):
                            lag_out[0, j, pl.ds(at, 16), sl] = q[j].astype(jnp.bfloat16)
                            lag_out[1, j, pl.ds(at, 16), sl] = one[j].astype(jnp.bfloat16)

            @pl.loop(0, 16)
            def _(r):
                for sl in blocks:
                    s = s_ref[i * 16 + r, :, sl]
                    for turn in range(STEPS):
                        s = pole_ref[:, sl] * s + ps[turn, pl.ds(r, 1), sl]
                        ys[turn, pl.ds(r, 1), sl] = jnp.sum(res_ref[:, sl] * s, axis=0, keepdims=True)
                        if turn < STEPS - 1:
                            s = s * alive(turn, at + r)
                    s_ref[i * 16 + r, :, sl] = s

            for turn in range(STEPS):
                g_ref[pl.ds(pl.multiple_of(turn * rows + i * 16, 16), 16), :] = (
                    xs[turn] * (ys[turn] + skip_ref[...] * ps[turn])
                ).astype(jnp.bfloat16)

    def near_copy(c, s):
        gap = jnp.abs(s - z)
        slot = jnp.where(s > z, 0, 2) + jnp.minimum(gap, 2) - 1
        return pltpu.make_async_remote_copy(
            src_ref=p_refs[c].at[s],
            dst_ref=r_refs[c].at[slot],
            send_sem=rs_sem.at[c, s],
            recv_sem=rr_sem.at[c, slot],
            device_id={"tensor": s},
            device_id_type=MESH,
        )

    def far_copy(c, s):
        return pltpu.make_async_remote_copy(
            src_ref=p_refs[c].at[s],
            dst_ref=relay_refs[c].at[s],
            send_sem=rs_sem.at[c, s],
            recv_sem=rl_sem.at[c, s],
            device_id={"tensor": jnp.where(s > z, z + 1, z - 1)},
            device_id_type=MESH,
        )

    def send_part(c, s):
        gap = jnp.abs(s - z)

        @pl.when(gap <= 2)
        def _():
            near_copy(c, s).start()

        @pl.when(gap > 2)
        def _():
            far_copy(c, s).start()

    def owner_at(i):
        return jnp.where(2 * z < shards, shards - 1 - i, i)

    def relays(s):
        behind = jnp.where(s > z, z > 0, z < shards - 1)
        return jnp.logical_and(jnp.abs(s - z) >= 2, behind)

    def product(c, s):
        return jnp.dot(
            g_refs[c][...],
            w_ref[:, pl.ds(pl.multiple_of(s * cols, cols), cols)],
            preferred_element_type=jnp.float32,
        )

    def project(c):
        @pl.loop(0, shards)
        def _(i):
            s = owner_at(i)

            @pl.when(jnp.logical_and(s != z, jnp.logical_not(relays(s))))
            def _():
                p_refs[c][s] = product(c, s).astype(jnp.bfloat16)
                send_part(c, s)

        t_refs[c][...] = product(c, z)

    def relay(c):
        @pl.loop(0, shards)
        def _(i):
            s = owner_at(i)

            @pl.when(jnp.logical_and(s != z, relays(s)))
            def _():
                part = product(c, s)
                far_copy(c, s).wait_recv()
                p_refs[c][s] = (part + relay_refs[c][s].astype(jnp.float32)).astype(jnp.bfloat16)
                send_part(c, s)

    here = [z >= 1, z >= 2, z <= shards - 2, z <= shards - 3]

    def pieces(rows):
        return [(i, min(128, rows - i)) for i in range(0, rows, 128)]

    def eye(size):
        return lax.broadcasted_iota(jnp.int32, (size, 128), 0) == lax.broadcasted_iota(
            jnp.int32, (size, 128), 1
        )

    def square_copy(c, j):
        return pltpu.make_async_remote_copy(
            src_ref=ss_own.at[c],
            dst_ref=ss_recv.at[c, j],
            send_sem=ss_sem.at[c, j],
            recv_sem=sr_sem.at[c, j],
            device_id={"tensor": lax.rem(z + j, shards)},
            device_id_type=MESH,
        )

    def collect(c):
        r_ref, t_ref = r_refs[c], t_refs[c]
        for slot in range(4):
            @pl.when(here[slot])
            def _():
                pltpu.make_async_remote_copy(
                    src_ref=r_ref.at[slot],
                    dst_ref=r_ref.at[slot],
                    send_sem=rs_sem.at[c, 0],
                    recv_sem=rr_sem.at[c, slot],
                    device_id={"tensor": lax.rem(z + 1, shards)},
                    device_id_type=MESH,
                ).wait_recv()
                t_ref[...] += r_ref[slot].astype(jnp.float32)

        for at, (i, size) in enumerate(pieces(t_ref.shape[0])):
            x = t_ref[i : i + size, :]
            squares = jnp.sum(x * x, axis=1, keepdims=True)
            ss_own[c, at : at + 1, :] = jnp.sum(
                jnp.where(eye(size), squares, 0.0), axis=0, keepdims=True
            )
        for j in range(1, shards):
            square_copy(c, j).start()

    def finish(c):
        t_ref, rows, first = t_refs[c], chunks[c % nc], firsts[c % nc]
        turn_at = STEPS - 1 if c == 0 else 0
        for j in range(1, shards):
            square_copy(c, j).wait_recv()
        total = ss_own[c]
        for j in range(1, shards):
            total = total + ss_recv[c, j]
        for at, (i, size) in enumerate(pieces(t_ref.shape[0])):
            squares = jnp.sum(jnp.where(eye(size), total[at : at + 1], 0.0), axis=1, keepdims=True)
            scale = lax.rsqrt(squares / (cols * shards) + 1e-05)
            value = (t_ref[i : i + size, :] * scale * gain_ref[...]).astype(jnp.bfloat16)
            for turn in range(i // rows, (i + size) // rows):
                part = turn * rows - i
                mix_out[turn_at + turn, first : first + rows, :] = value[part : part + rows]

    def stay(c):
        loads[c].wait()
        staying(c)
        stores[c].start()
        if c == 1:
            load_w.wait()
        project(c)

    for load in small_loads:
        load.wait()
    loads[0].wait()
    moving_step(0)
    pl.semaphore_wait(barrier, groups + shards - 2)
    send_moving(0)
    moving_gate(0)
    stay(1)
    await_moving(0)
    moving_step(1)
    send_moving(1)
    moving_gate(1)
    relay(1)
    for c in range(2, nc):
        stay(c)
    await_moving(1)
    moving_step(2)
    send_moving(2)
    moving_gate(2)
    project(nc)
    for c in range(2, nc):
        relay(c)
    await_moving(2)
    moving_step(3)
    moving_gate(3)
    stores[0].start()
    project(0)
    relay(nc)
    collect(1)
    relay(0)
    for c in range(2, nc + 1):
        collect(c)
    for c in range(1, nc + 1):
        finish(c)
    collect(0)
    finish(0)
    for turn in range(STEPS - 1):
        @pl.loop(1, groups)
        def _(d):
            migration(turn, d).wait_send()
    for c in range(nc + 1):
        @pl.loop(0, shards)
        def _(s):
            @pl.when(s != z)
            def _():
                near_copy(c, s).wait_send()

        for j in range(1, shards):
            square_copy(c, j).wait_send()
    for store in stores:
        store.wait()


def per_device(
    qkv,
    fir_buffer,
    fir_taps,
    modal_state,
    poles,
    residues,
    skip,
    out_weight,
    norm_gain,
    finished,
    dest_group,
):
    groups = lax.axis_size("dp")
    shards = lax.axis_size("tensor")
    rows, order, chans = modal_state.shape
    cols = norm_gain.shape[0]
    f32 = jnp.float32
    bf16 = jnp.bfloat16

    moving = groups * CAP
    left = rows - moving
    half = left // 32 * 16
    chunks = (moving,) + ((half, left - half) if half else (left,))
    nc = len(chunks)
    tall = [moving] + [STEPS * n for n in chunks[1:]] + [(STEPS - 1) * moving]
    vmem = pl.BlockSpec(memory_space=pltpu.VMEM)
    smem = pl.BlockSpec(memory_space=pltpu.SMEM)
    anywhere = pl.BlockSpec(memory_space=pl.ANY)
    hbm = pl.BlockSpec(memory_space=pltpu.HBM)
    dma = pltpu.SemaphoreType.DMA
    small = (qkv.transpose(0, 2, 1, 3), fir_taps, poles, residues, skip[None], norm_gain[None])
    pin = functools.partial(pltpu.with_memory_space_constraint, memory_space=pltpu.HBM)
    small = tuple(pin(x) for x in small)
    modal_state, out_weight, finished, dest_group = map(
        pin, (modal_state, out_weight, finished, dest_group)
    )
    outs = pl.pallas_call(
        functools.partial(kernel, groups, shards, chunks),
        out_shape=[
            jax.ShapeDtypeStruct((STEPS, rows, cols), bf16),
            jax.ShapeDtypeStruct(modal_state.shape, f32),
            jax.ShapeDtypeStruct((2, 3, rows, chans), bf16),
        ],
        in_specs=[vmem] * 2 + [hbm] * 8 + [smem] * 2,
        out_specs=[vmem, anywhere, vmem],
        scratch_shapes=[pltpu.VMEM((n, order, chans), f32) for n in chunks]
        + [pltpu.VMEM(x.shape, x.dtype) for x in small]
        + [
            pltpu.VMEM(out_weight.shape, bf16),
            pltpu.VMEM((2, 3, moving, chans), f32),
            pltpu.VMEM((groups, 16, chans), f32),
            pltpu.VMEM((STEPS - 1, groups, 48, chans), bf16),
        ]
        + [pltpu.VMEM((groups, 48, chans), bf16)] * (STEPS - 1)
        + [pltpu.VMEM((moving, chans), f32)] * 3
        + [pltpu.VMEM((STEPS, 16, chans), f32)] * 3
        + [pltpu.VMEM((n, chans), bf16) for n in tall]
        + [pltpu.VMEM((shards, n, cols), bf16) for n in tall]
        + [pltpu.VMEM((4, n, cols), bf16) for n in tall]
        + [pltpu.VMEM((shards, n, cols), bf16) for n in tall]
        + [pltpu.VMEM((n, cols), f32) for n in tall]
        + [
            pltpu.VMEM((nc + 1, 8, 128), f32),
            pltpu.VMEM((nc + 1, shards, 8, 128), f32),
            dma((nc + 7,)),
            dma((nc,)),
            dma((STEPS - 1, groups)),
            dma((STEPS - 1, groups)),
            dma((nc + 1, shards)),
            dma((nc + 1, 4)),
            dma((nc + 1, shards)),
            dma((nc + 1, shards)),
            dma((nc + 1, shards)),
        ],
        compiler_params=pltpu.CompilerParams(
            collective_id=0, has_side_effects=True, vmem_limit_bytes=38 * 1024 * 1024
        ),
        name="mixer",
    )(
        fir_buffer.transpose(2, 1, 0, 3),
        finished,
        modal_state,
        out_weight,
        *small,
        finished,
        dest_group,
    )
    mixed, state, lagged = outs
    return (mixed, state, lagged.transpose(2, 1, 0, 3))


def solution(mesh):
    return jax.shard_map(
        per_device,
        mesh=mesh,
        in_specs=(
            P(None, "dp", None, "tensor"),
            P("dp", None, None, "tensor"),
            P(None, None, "tensor"),
            P("dp", None, "tensor"),
            P(None, "tensor"),
            P(None, "tensor"),
            P("tensor"),
            P("tensor", None),
            P("tensor"),
            P(None, "dp"),
            P(None, "dp"),
        ),
        out_specs=(P(None, "dp", "tensor"), P("dp", None, "tensor"), P("dp", None, None, "tensor")),
        check_vma=False,
    )
```

```python
import functools

import jax
import jax.numpy as jnp
from jax import lax
from jax.experimental import pallas as pl
from jax.experimental.pallas import tpu as pltpu
from jax.sharding import PartitionSpec as P

STEPS = 4
CAP = 2
MESH = pl.DeviceIdType.MESH
LANES = 512


def row_update(poles, res, skip, s, x, p):
    s = poles * s + p
    y = jnp.sum(res * s, axis=0, keepdims=True) + skip * p
    return s, x * y


def kernel(groups, shards, chunks, *refs):
    refs = list(refs)

    def take(count):
        got = refs[:count]
        del refs[:count]
        return got

    nc = len(chunks)
    l_ref, fin_ref, st_ref, w_hbm = take(4)
    small_hbm = take(6)
    done_ref, dest_ref = take(2)
    mix_out, st_out, lag_out = take(3)
    s_refs = take(nc)
    small_refs = take(6)
    q_ref, tap_ref, pole_ref, res_ref, skip_ref, gain_ref = small_refs
    w_ref, lagn, lagm, msend = take(4)
    mrecv = take(STEPS - 1)
    xm, pm, ym, xs, ps, ys = take(6)
    np = nc + 1
    g_refs, p_refs, r_refs, relay_refs, t_refs = take(np), take(np), take(np), take(np), take(np)
    ss_own, ss_recv = take(2)
    load_sem, store_sem, ms_sem, mr_sem, rs_sem, rr_sem, rl_sem, ss_sem, sr_sem = take(9)
    sm = s_refs[0]
    me = lax.axis_index("dp")
    z = lax.axis_index("tensor")
    cols = gain_ref.shape[1]
    chans = pole_ref.shape[1]
    lanes = min(LANES, chans)
    blocks = [slice(i, i + lanes) for i in range(0, chans, lanes)]
    bands_m = chunks[0] // CAP
    firsts = [sum(chunks[:c]) for c in range(nc)]

    barrier = pltpu.get_barrier_semaphore()

    @pl.loop(1, groups)
    def _(d):
        pl.semaphore_signal(barrier, inc=1, device_id={"dp": lax.rem(me + d, groups)}, device_id_type=MESH)

    @pl.loop(1, shards)
    def _(d):
        pl.semaphore_signal(barrier, inc=1, device_id={"tensor": lax.rem(z + d, shards)}, device_id_type=MESH)

    loads = [
        pltpu.make_async_copy(st_ref.at[pl.ds(firsts[c], chunks[c])], s_refs[c], load_sem.at[c])
        for c in range(nc)
    ]
    load_w = pltpu.make_async_copy(w_hbm, w_ref, load_sem.at[nc])
    stores = [
        pltpu.make_async_copy(s_refs[c], st_out.at[pl.ds(firsts[c], chunks[c])], store_sem.at[c])
        for c in range(nc)
    ]
    small_loads = [
        pltpu.make_async_copy(small_hbm[i], small_refs[i], load_sem.at[nc + 1 + i]) for i in range(6)
    ]
    for load in small_loads:
        load.start()
    loads[1].start()
    load_w.start()
    loads[0].start()
    for load in loads[2:]:
        load.start()
    ss_own[...] = jnp.zeros_like(ss_own)
    lagm[...] = jnp.zeros_like(lagm)

    def migration(turn, d):
        return pltpu.make_async_remote_copy(
            src_ref=msend.at[turn, d],
            dst_ref=mrecv[turn].at[d],
            send_sem=ms_sem.at[turn, d],
            recv_sem=mr_sem.at[turn, d],
            device_id={"dp": lax.rem(me + d, groups)},
            device_id_type=MESH,
        )

    def alive(turn, row):
        return (1 - done_ref[turn, row]).astype(jnp.float32)

    def alive_column(turn, at):
        shape = (16, fin_ref.shape[1])
        row = lax.broadcasted_iota(jnp.int32, shape, 0) + at
        lane = lax.broadcasted_iota(jnp.int32, shape, 1)
        flags = (1 - fin_ref[turn : turn + 1, :]).astype(jnp.float32)
        return jnp.sum(jnp.where(row == lane, flags, 0.0), axis=1, keepdims=True)

    def taken(sl, q, one, two):
        return [
            tap_ref[j, 0:1, sl] * q[j] + tap_ref[j, 1:2, sl] * one[j] + tap_ref[j, 2:3, sl] * two[j]
            for j in range(3)
        ]

    def moving_step(turn):
        if turn > 0:
            @pl.loop(0, chunks[0] // 8)
            def _(i):
                lags = []
                for u in range(8 // CAP):
                    k = lax.rem(dest_ref[turn - 1, i * 8 + u * CAP] - me + groups, groups)
                    lags.append(mrecv[turn - 1][k, 32:48, :].astype(jnp.float32))
                for l in range(2):
                    for j in range(3):
                        at = l * 8 + j * CAP
                        lagn[l, j, pl.ds(pl.multiple_of(i * 8, 8), 8), :] = jnp.concatenate(
                            [lag[at : at + CAP] for lag in lags], axis=0
                        )

        @pl.loop(0, chunks[0] // 16)
        def _(i):
            rows = pl.ds(pl.multiple_of(i * 16, 16), 16)
            mask = alive_column(turn, i * 16) if turn < STEPS - 1 else None

            @pl.loop(0, chans // 128)
            def _(block):
                sl = pl.ds(pl.multiple_of(block * 128, 128), 128)
                lag_ref = lagn if turn > 0 else l_ref
                one = [lag_ref[0, j, rows, sl].astype(jnp.float32) for j in range(3)]
                two = [lag_ref[1, j, rows, sl].astype(jnp.float32) for j in range(3)]
                q = [q_ref[turn, j, rows, sl].astype(jnp.float32) for j in range(3)]
                f = taken(sl, q, one, two)
                xm[rows, sl] = f[0]
                pm[rows, sl] = f[1] * f[2]
                for j in range(3):
                    if turn < STEPS - 1:
                        lagn[0, j, rows, sl] = q[j] * mask
                        lagn[1, j, rows, sl] = one[j] * mask
                    else:
                        lag_out[0, j, rows, sl] = q[j].astype(jnp.bfloat16)
                        lag_out[1, j, rows, sl] = one[j].astype(jnp.bfloat16)

        @pl.loop(0, bands_m)
        def _(b):
            if turn > 0:
                k = lax.rem(dest_ref[turn - 1, b * CAP] - me + groups, groups)
            for r in range(CAP):
                row = b * CAP + r
                for sl in blocks:
                    if turn > 0:
                        s = mrecv[turn - 1][k, 16 * r : 16 * r + 16, sl].astype(jnp.float32)
                    else:
                        s = sm[row, :, sl]
                    s = pole_ref[:, sl] * s + pm[pl.ds(row, 1), sl]
                    ym[pl.ds(row, 1), sl] = jnp.sum(res_ref[:, sl] * s, axis=0, keepdims=True)
                    if turn < STEPS - 1:
                        s = s * alive(turn, row)
                    sm[row, :, sl] = s

        if turn < STEPS - 1:
            @pl.loop(0, chunks[0] // 8)
            def _(i):
                for l in range(2):
                    for j in range(3):
                        at = l * 8 + j * CAP
                        lag = lagn[l, j, pl.ds(pl.multiple_of(i * 8, 8), 8), :]
                        for u in range(8 // CAP):
                            lagm[i * (8 // CAP) + u, at : at + CAP, :] = lag[u * CAP : u * CAP + CAP]

    def moving_gate(turn):
        g_ref, at = (g_refs[nc], turn * chunks[0]) if turn < STEPS - 1 else (g_refs[0], 0)
        g_ref[at : at + chunks[0], :] = (
            xm[...] * (ym[...] + skip_ref[...] * pm[...])
        ).astype(jnp.bfloat16)

    def pack(turn, d, to_ref):
        target = lax.rem(me + d, groups)
        b = lax.fori_loop(
            0,
            bands_m,
            lambda i, found: jnp.where(dest_ref[turn, i * CAP] == target, i, found),
            jnp.int32(0),
        )
        for r in range(CAP):
            to_ref[16 * r : 16 * r + 16, :] = sm[b * CAP + r].astype(jnp.bfloat16)
        to_ref[32:48, :] = lagm[b].astype(jnp.bfloat16)

    def send_moving(turn):
        pack(turn, 0, mrecv[turn].at[0])

        @pl.loop(1, groups)
        def _(d):
            pack(turn, d, msend.at[turn, d])
            migration(turn, d).start()

    def await_moving(turn):
        @pl.loop(1, groups)
        def _(d):
            migration(turn, d).wait_recv()

    def staying(c):
        rows, first, s_ref, g_ref = chunks[c], firsts[c], s_refs[c], g_refs[c]

        @pl.loop(0, rows // 16)
        def _(i):
            at = pl.multiple_of(first + i * 16, 16)
            masks = [alive_column(turn, at) for turn in range(STEPS - 1)]

            @pl.loop(0, chans // 128)
            def _(block):
                sl = pl.ds(pl.multiple_of(block * 128, 128), 128)
                one = [l_ref[0, j, pl.ds(at, 16), sl].astype(jnp.float32) for j in range(3)]
                two = [l_ref[1, j, pl.ds(at, 16), sl].astype(jnp.float32) for j in range(3)]
                for turn in range(STEPS):
                    q = [q_ref[turn, j, pl.ds(at, 16), sl].astype(jnp.float32) for j in range(3)]
                    f = taken(sl, q, one, two)
                    xs[turn, :, sl] = f[0]
                    ps[turn, :, sl] = f[1] * f[2]
                    if turn < STEPS - 1:
                        two = [v * masks[turn] for v in one]
                        one = [v * masks[turn] for v in q]
                    else:
                        for j in range(3):
                            lag_out[0, j, pl.ds(at, 16), sl] = q[j].astype(jnp.bfloat16)
                            lag_out[1, j, pl.ds(at, 16), sl] = one[j].astype(jnp.bfloat16)

            @pl.loop(0, 16)
            def _(r):
                for sl in blocks:
                    s = s_ref[i * 16 + r, :, sl]
                    for turn in range(STEPS):
                        s = pole_ref[:, sl] * s + ps[turn, pl.ds(r, 1), sl]
                        ys[turn, pl.ds(r, 1), sl] = jnp.sum(res_ref[:, sl] * s, axis=0, keepdims=True)
                        if turn < STEPS - 1:
                            s = s * alive(turn, at + r)
                    s_ref[i * 16 + r, :, sl] = s

            for turn in range(STEPS):
                g_ref[pl.ds(pl.multiple_of(turn * rows + i * 16, 16), 16), :] = (
                    xs[turn] * (ys[turn] + skip_ref[...] * ps[turn])
                ).astype(jnp.bfloat16)

    def near_copy(c, s):
        gap = jnp.abs(s - z)
        slot = jnp.where(s > z, 0, 2) + jnp.minimum(gap, 2) - 1
        return pltpu.make_async_remote_copy(
            src_ref=p_refs[c].at[s],
            dst_ref=r_refs[c].at[slot],
            send_sem=rs_sem.at[c, s],
            recv_sem=rr_sem.at[c, slot],
            device_id={"tensor": s},
            device_id_type=MESH,
        )

    def far_copy(c, s):
        return pltpu.make_async_remote_copy(
            src_ref=p_refs[c].at[s],
            dst_ref=relay_refs[c].at[s],
            send_sem=rs_sem.at[c, s],
            recv_sem=rl_sem.at[c, s],
            device_id={"tensor": jnp.where(s > z, z + 1, z - 1)},
            device_id_type=MESH,
        )

    def send_part(c, s):
        gap = jnp.abs(s - z)

        @pl.when(gap <= 2)
        def _():
            near_copy(c, s).start()

        @pl.when(gap > 2)
        def _():
            far_copy(c, s).start()

    def owner_at(i):
        return jnp.where(2 * z < shards, shards - 1 - i, i)

    def relays(s):
        behind = jnp.where(s > z, z > 0, z < shards - 1)
        return jnp.logical_and(jnp.abs(s - z) >= 2, behind)

    def product(c, s):
        return jnp.dot(
            g_refs[c][...],
            w_ref[:, pl.ds(pl.multiple_of(s * cols, cols), cols)],
            preferred_element_type=jnp.float32,
        )

    def project(c):
        @pl.loop(0, shards)
        def _(i):
            s = owner_at(i)

            @pl.when(jnp.logical_and(s != z, jnp.logical_not(relays(s))))
            def _():
                p_refs[c][s] = product(c, s).astype(jnp.bfloat16)
                send_part(c, s)

        t_refs[c][...] = product(c, z)

    def relay(c):
        @pl.loop(0, shards)
        def _(i):
            s = owner_at(i)

            @pl.when(jnp.logical_and(s != z, relays(s)))
            def _():
                part = product(c, s)
                far_copy(c, s).wait_recv()
                p_refs[c][s] = (part + relay_refs[c][s].astype(jnp.float32)).astype(jnp.bfloat16)
                send_part(c, s)

    here = [z >= 1, z >= 2, z <= shards - 2, z <= shards - 3]

    def pieces(c):
        rows, step = t_refs[c].shape[0], 128 // chunks[c % nc] * chunks[c % nc]
        return [(i, min(step, rows - i)) for i in range(0, rows, step)]

    def eye(size):
        return lax.broadcasted_iota(jnp.int32, (size, 128), 0) == lax.broadcasted_iota(
            jnp.int32, (size, 128), 1
        )

    def square_copy(c, j):
        return pltpu.make_async_remote_copy(
            src_ref=ss_own.at[c],
            dst_ref=ss_recv.at[c, j],
            send_sem=ss_sem.at[c, j],
            recv_sem=sr_sem.at[c, j],
            device_id={"tensor": lax.rem(z + j, shards)},
            device_id_type=MESH,
        )

    def collect(c):
        r_ref, t_ref = r_refs[c], t_refs[c]
        for slot in range(4):
            @pl.when(here[slot])
            def _():
                pltpu.make_async_remote_copy(
                    src_ref=r_ref.at[slot],
                    dst_ref=r_ref.at[slot],
                    send_sem=rs_sem.at[c, 0],
                    recv_sem=rr_sem.at[c, slot],
                    device_id={"tensor": lax.rem(z + 1, shards)},
                    device_id_type=MESH,
                ).wait_recv()
                t_ref[...] += r_ref[slot].astype(jnp.float32)

        for at, (i, size) in enumerate(pieces(c)):
            x = t_ref[i : i + size, :]
            squares = jnp.sum(x * x, axis=1, keepdims=True)
            ss_own[c, at : at + 1, :] = jnp.sum(
                jnp.where(eye(size), squares, 0.0), axis=0, keepdims=True
            )
        for j in range(1, shards):
            square_copy(c, j).start()

    def finish(c):
        t_ref, rows, first = t_refs[c], chunks[c % nc], firsts[c % nc]
        turn_at = STEPS - 1 if c == 0 else 0
        for j in range(1, shards):
            square_copy(c, j).wait_recv()
        total = ss_own[c]
        for j in range(1, shards):
            total = total + ss_recv[c, j]
        for at, (i, size) in enumerate(pieces(c)):
            squares = jnp.sum(jnp.where(eye(size), total[at : at + 1], 0.0), axis=1, keepdims=True)
            scale = lax.rsqrt(squares / (cols * shards) + 1e-05)
            value = (t_ref[i : i + size, :] * scale * gain_ref[...]).astype(jnp.bfloat16)
            for turn in range(i // rows, (i + size) // rows):
                part = turn * rows - i
                mix_out[turn_at + turn, first : first + rows, :] = value[part : part + rows]

    def stay(c):
        loads[c].wait()
        staying(c)
        stores[c].start()
        if c == 1:
            load_w.wait()
            pl.semaphore_wait(barrier, groups + shards - 2)
        project(c)

    for load in small_loads:
        load.wait()
    stay(1)
    loads[0].wait()
    moving_step(0)
    send_moving(0)
    moving_gate(0)
    for c in range(2, nc):
        stay(c)
    await_moving(0)
    moving_step(1)
    send_moving(1)
    moving_gate(1)
    relay(1)
    await_moving(1)
    moving_step(2)
    send_moving(2)
    moving_gate(2)
    project(nc)
    for c in range(2, nc):
        relay(c)
    await_moving(2)
    moving_step(3)
    moving_gate(3)
    stores[0].start()
    project(0)
    relay(nc)
    collect(1)
    relay(0)
    for c in range(2, nc + 1):
        collect(c)
    for c in range(1, nc + 1):
        finish(c)
    collect(0)
    finish(0)
    for turn in range(STEPS - 1):
        @pl.loop(1, groups)
        def _(d):
            migration(turn, d).wait_send()
    for c in range(nc + 1):
        @pl.loop(0, shards)
        def _(s):
            @pl.when(s != z)
            def _():
                near_copy(c, s).wait_send()

        for j in range(1, shards):
            square_copy(c, j).wait_send()
    for store in stores:
        store.wait()


def per_device(
    qkv,
    fir_buffer,
    fir_taps,
    modal_state,
    poles,
    residues,
    skip,
    out_weight,
    norm_gain,
    finished,
    dest_group,
):
    groups = lax.axis_size("dp")
    shards = lax.axis_size("tensor")
    rows, order, chans = modal_state.shape
    cols = norm_gain.shape[0]
    f32 = jnp.float32
    bf16 = jnp.bfloat16

    moving = groups * CAP
    left = rows - moving
    half = 16 if left > 16 else 0
    chunks = (moving,) + ((half, left - half) if half else (left,))
    nc = len(chunks)
    tall = [moving] + [STEPS * n for n in chunks[1:]] + [(STEPS - 1) * moving]
    vmem = pl.BlockSpec(memory_space=pltpu.VMEM)
    smem = pl.BlockSpec(memory_space=pltpu.SMEM)
    anywhere = pl.BlockSpec(memory_space=pl.ANY)
    hbm = pl.BlockSpec(memory_space=pltpu.HBM)
    dma = pltpu.SemaphoreType.DMA
    small = (qkv.transpose(0, 2, 1, 3), fir_taps, poles, residues, skip[None], norm_gain[None])
    pin = functools.partial(pltpu.with_memory_space_constraint, memory_space=pltpu.HBM)
    small = tuple(pin(x) for x in small)
    modal_state, out_weight, finished, dest_group = map(
        pin, (modal_state, out_weight, finished, dest_group)
    )
    outs = pl.pallas_call(
        functools.partial(kernel, groups, shards, chunks),
        out_shape=[
            jax.ShapeDtypeStruct((STEPS, rows, cols), bf16),
            jax.ShapeDtypeStruct(modal_state.shape, f32),
            jax.ShapeDtypeStruct((2, 3, rows, chans), bf16),
        ],
        in_specs=[vmem] * 2 + [hbm] * 8 + [smem] * 2,
        out_specs=[vmem, anywhere, vmem],
        scratch_shapes=[pltpu.VMEM((n, order, chans), f32) for n in chunks]
        + [pltpu.VMEM(x.shape, x.dtype) for x in small]
        + [
            pltpu.VMEM(out_weight.shape, bf16),
            pltpu.VMEM((2, 3, moving, chans), f32),
            pltpu.VMEM((groups, 16, chans), f32),
            pltpu.VMEM((STEPS - 1, groups, 48, chans), bf16),
        ]
        + [pltpu.VMEM((groups, 48, chans), bf16)] * (STEPS - 1)
        + [pltpu.VMEM((moving, chans), f32)] * 3
        + [pltpu.VMEM((STEPS, 16, chans), f32)] * 3
        + [pltpu.VMEM((n, chans), bf16) for n in tall]
        + [pltpu.VMEM((shards, n, cols), bf16) for n in tall]
        + [pltpu.VMEM((4, n, cols), bf16) for n in tall]
        + [pltpu.VMEM((shards, n, cols), bf16) for n in tall]
        + [pltpu.VMEM((n, cols), f32) for n in tall]
        + [
            pltpu.VMEM((nc + 1, 8, 128), f32),
            pltpu.VMEM((nc + 1, shards, 8, 128), f32),
            dma((nc + 7,)),
            dma((nc,)),
            dma((STEPS - 1, groups)),
            dma((STEPS - 1, groups)),
            dma((nc + 1, shards)),
            dma((nc + 1, 4)),
            dma((nc + 1, shards)),
            dma((nc + 1, shards)),
            dma((nc + 1, shards)),
        ],
        compiler_params=pltpu.CompilerParams(
            collective_id=0, has_side_effects=True, vmem_limit_bytes=38 * 1024 * 1024
        ),
        name="mixer",
    )(
        fir_buffer.transpose(2, 1, 0, 3),
        finished,
        modal_state,
        out_weight,
        *small,
        finished,
        dest_group,
    )
    mixed, state, lagged = outs
    return (mixed, state, lagged.transpose(2, 1, 0, 3))


def solution(mesh):
    return jax.shard_map(
        per_device,
        mesh=mesh,
        in_specs=(
            P(None, "dp", None, "tensor"),
            P("dp", None, None, "tensor"),
            P(None, None, "tensor"),
            P("dp", None, "tensor"),
            P(None, "tensor"),
            P(None, "tensor"),
            P("tensor"),
            P("tensor", None),
            P("tensor"),
            P(None, "dp"),
            P(None, "dp"),
        ),
        out_specs=(P(None, "dp", "tensor"), P("dp", None, "tensor"), P("dp", None, None, "tensor")),
        check_vma=False,
    )
```
